512 devices in a mesh: space: 64 (over x, y, z_hi), dp: 8 (over z_lo, core).
Axes of the slice: x: 4, y: 8, z: 8 (z_hi: 2, z_lo: 4; z = z_hi * 4 + z_lo), core: 2. Of those that a mesh axis runs over, the one named last changes fastest.
Arguments:
- volume: bfloat16 [8, 128, 16, 256], P('dp', 'space'), may hold values from -6 to 6
- weight: bfloat16 [1728, 128], replicated, may hold values from -0.15625 to 0.15625
- cotangent: bfloat16 [8, 128, 16, 512], P('dp', 'space'), may hold values from -6 to 6
- left_stat: float32 [1728, 1728], P('dp'), may hold values from -27648 to 27648, as said below
- right_stat: float32 [128, 128], replicated, may hold values from -27648 to 27648, as said below
Outputs:
- output: bfloat16 [8, 128, 16, 512], P('dp', 'space')
- input_grad: bfloat16 [8, 128, 16, 256], P('dp', 'space')
- gradient: float32 [1728, 128], replicated
- direction: float32 [1728, 128], P('dp')
The draws below stay inside these ranges and needn't reach their ends.
Inputs may be any that keep to these rules, and one draw needn't show every extreme that they name: `left_stat`: symmetric positive definite. `right_stat`: symmetric positive definite.
All inputs are finite; a program needn't handle non-finite values.
Results may differ from the reference program's by a relative error of at most 0.0049.
Values may be sent and summed in bfloat16 or wider, within the bound.
No kernel may reach another device: no remote copies, remote signals or barrier semaphores. Data moves between devices by JAX's collectives and lax.ppermute only.
A program may use at most 64 MiB of HBM per device.

```python
import math
import jax
import jax.numpy as jnp
from jax import lax

CIN = 64
COUT = 128
NX = 4
NY = 16
POWER = 4
FAN = 1728
SAMPLES = 8
DEPTH = 128
VOXELS = 65536


def draw_statistic(key, dimension, spread, span):
    first_key = jax.random.fold_in(key, 0)
    factor = jax.random.normal(first_key, (dimension, 2 * dimension), jnp.float32) * spread
    statistic = jnp.dot(factor, factor.T, precision=lax.Precision.HIGHEST)
    position = jnp.arange(dimension, dtype=jnp.float32) / dimension
    scales = jnp.exp(math.log(span) * (position - 1.0))
    statistic = statistic * scales[:, None] * scales[None, :]
    return 0.5 * (statistic + statistic.T)


def draw_left_stat(key, part):
    key = jax.random.fold_in(key, 11)
    span = 30.0
    return draw_statistic(key, FAN, 0.5, span)


def draw_right_stat(key, part):
    key = jax.random.fold_in(key, 23)
    return draw_statistic(key, COUT, 0.6 * math.sqrt(FAN / (2.0 * COUT)), 1.0)


def block_levels(stream_key, extent, cuts, least, high):
    def one(axis_at, parts):
        heights = jax.random.uniform(jax.random.fold_in(jax.random.fold_in(stream_key, 6), axis_at), (parts,), jnp.float32, least / len(cuts), high / len(cuts))
        return jnp.repeat(jnp.exp(heights), extent[axis_at] // parts).reshape((-1,) + (1,) * (len(extent) - axis_at - 1))

    loudness = one(*cuts[0])
    for cut in cuts[1:]:
        loudness = loudness * one(*cut)
    return loudness


def bell_draw(stream_key, dims, deviation, most, pieces=(), held_as=jnp.bfloat16):
    entries = deviation * jax.random.normal(stream_key, dims, jnp.float32)
    if pieces:
        entries = entries * block_levels(stream_key, dims, pieces, -0.22, 0.18)
    return jnp.clip(entries, -most, most).astype(held_as)


def setup_inputs(seed: int = 0) -> dict:
    key_of = jax.random.split(jax.random.key(seed), 6)
    volume = bell_draw(key_of[0], (SAMPLES, DEPTH, NY, NX * CIN), 1.0, 6.0, ((0, 8), (1, 64)))
    weight = bell_draw(key_of[1], (FAN, COUT), FAN ** -0.5, 0.15625)
    cotangent = bell_draw(key_of[2], (SAMPLES, DEPTH, NY, NX * COUT), 1.0, 6.0, ((0, 8), (1, 64)))
    left_stat = draw_left_stat(jax.random.fold_in(key_of[5], 71), 0)
    right_stat = draw_right_stat(jax.random.fold_in(key_of[5], 71), 0)
    return dict(volume=volume, weight=weight, cotangent=cotangent, left_stat=left_stat, right_stat=right_stat)


DECAY = 0.9
EXACT_MODE = lax.Precision.HIGHEST

def offset_list():
    return [(a, b, c) for a in (-1, 0, 1) for b in (-1, 0, 1) for c in (-1, 0, 1)]

def root_coefficients():
    terms_list = [(1, 5.0), (5, -5.0), (6, 4.0)]
    coeffs = [0.0] * 7
    for degree, factor in terms_list:
        for j in range(degree + 1):
            coeffs[j] += factor * math.comb(degree, j) * 1.25 ** (degree - j) * (-0.25) ** j / 4.0
    return coeffs

def top_scale(matrix):
    dimension = matrix.shape[0]
    vector = jnp.full((dimension,), 1.0 / math.sqrt(dimension), jnp.float32)
    length = jnp.float32(1.0)
    for repeat in range(POWER):
        product = jnp.dot(matrix, vector, precision=EXACT_MODE)
        length = jnp.sqrt(jnp.sum(product * product))
        vector = product / length
    return length

def small_root(matrix):
    largest = top_scale(matrix)
    unit_matrix = matrix / largest
    coeffs = root_coefficients()
    identity = jnp.eye(matrix.shape[0], dtype=jnp.float32)
    summed = coeffs[0] * identity + coeffs[1] * unit_matrix
    current = unit_matrix
    for degree in range(2, 7):
        current = jnp.dot(current, unit_matrix, precision=EXACT_MODE)
        summed = summed + coeffs[degree] * current
    return summed * largest ** (-0.25)

def reference(volume, weight, cotangent, left_stat, right_stat):
    cells_grid = volume.reshape(SAMPLES, DEPTH, NY, NX, CIN)
    weight_blocks = weight.reshape(27, CIN, COUT)
    offsets = offset_list()
    preact = jnp.zeros((SAMPLES * DEPTH * NY * NX, COUT), jnp.float32)
    for k in range(27):
        a, b, c = offsets[k]
        moved = jnp.roll(cells_grid, (-a, -b, -c), axis=(1, 2, 3)).reshape(-1, CIN)
        preact = preact + jnp.dot(moved, weight_blocks[k], preferred_element_type=jnp.float32)
    sigmoid_val = jax.nn.sigmoid(preact)
    output = (preact * sigmoid_val).astype(jnp.bfloat16).reshape(SAMPLES, DEPTH, NY, NX * COUT)
    upstream = cotangent.reshape(-1, COUT).astype(jnp.float32)
    pre_grad = (upstream * sigmoid_val * (1.0 + preact * (1.0 - sigmoid_val))).astype(jnp.bfloat16)
    grad_grid = pre_grad.reshape(SAMPLES, DEPTH, NY, NX, COUT)
    input_acc = jnp.zeros((SAMPLES * DEPTH * NY * NX, CIN), jnp.float32)
    blocks_list = []
    for k in range(27):
        a, b, c = offsets[k]
        moved = jnp.roll(cells_grid, (-a, -b, -c), axis=(1, 2, 3)).reshape(-1, CIN)
        blocks_list.append(jnp.dot(moved.T, pre_grad, preferred_element_type=jnp.float32))
        back = jnp.roll(grad_grid, (a, b, c), axis=(1, 2, 3)).reshape(-1, COUT)
        input_acc = input_acc + jnp.dot(back, weight_blocks[k].T, preferred_element_type=jnp.float32)
    input_grad = input_acc.astype(jnp.bfloat16).reshape(SAMPLES, DEPTH, NY, NX * CIN)
    gradient = jnp.concatenate(blocks_list, axis=0) / math.sqrt(VOXELS)
    left_full = DECAY * left_stat + jnp.dot(gradient, gradient.T, precision=EXACT_MODE)
    right_full = DECAY * right_stat + jnp.dot(gradient.T, gradient, precision=EXACT_MODE)
    largest = top_scale(left_full)
    unit_matrix = (left_full / largest).astype(jnp.bfloat16)
    coeffs = root_coefficients()
    identity = jnp.eye(FAN, dtype=jnp.float32)
    summed = coeffs[0] * identity + coeffs[1] * unit_matrix.astype(jnp.float32)
    current = unit_matrix
    for degree in range(2, 7):
        current = jnp.dot(current, unit_matrix, preferred_element_type=jnp.float32).astype(jnp.bfloat16)
        summed = summed + coeffs[degree] * current.astype(jnp.float32)
    left_root = summed * largest ** (-0.25)
    right_root = small_root(right_full)
    carried = jnp.dot(gradient, right_root, precision=EXACT_MODE)
    update = jnp.dot(left_root, carried, precision=EXACT_MODE)
    grad_norm = jnp.sqrt(jnp.sum(gradient * gradient))
    direction = update * grad_norm / (jnp.sqrt(jnp.sum(update * update)) + 1e-06)
    return (output, input_grad, gradient, direction)
```

```python
import math

import jax
import jax.numpy as jnp
from jax import lax
from jax.sharding import PartitionSpec as P

POWER = 4
DEGREE = 6


DECAY = 0.9
EXACT_MODE = lax.Precision.HIGHEST
EVERY = ("space", "dp")


def offset_list():
    return [(a, b, c) for a in (-1, 0, 1) for b in (-1, 0, 1) for c in (-1, 0, 1)]


def root_coefficients():
    terms_list = [(1, 5.0), (5, -5.0), (6, 4.0)]
    coeffs = [0.0] * 7
    for degree, factor in terms_list:
        for j in range(degree + 1):
            coeffs[j] += factor * math.comb(degree, j) * 1.25 ** (degree - j) * (-0.25) ** j / 4.0
    return coeffs


def top_scale(matrix):
    dimension = matrix.shape[0]
    vector = jnp.full((dimension,), 1.0 / math.sqrt(dimension), jnp.float32)
    length = jnp.float32(1.0)
    for repeat in range(POWER):
        product = jnp.dot(matrix, vector, precision=EXACT_MODE)
        length = jnp.sqrt(jnp.sum(product * product))
        vector = product / length
    return length


def small_root(matrix):
    largest = top_scale(matrix)
    unit_matrix = matrix / largest
    coeffs = root_coefficients()
    identity = jnp.eye(matrix.shape[0], dtype=jnp.float32)
    summed = coeffs[0] * identity + coeffs[1] * unit_matrix
    current = unit_matrix
    for degree in range(2, 7):
        current = jnp.dot(current, unit_matrix, precision=EXACT_MODE)
        summed = summed + coeffs[degree] * current
    return summed * largest ** (-0.25)


def gather_patches(padded, depth, channels, sign):
    leading = padded.shape[0]
    height = padded.shape[2]
    across = padded.shape[3] // channels
    pieces = []
    for a, b, c in offset_list():
        plane_block = lax.slice_in_dim(padded, 1 + sign * a, 1 + sign * a + depth, axis=1)
        plane_block = plane_block.reshape(leading, depth, height, across, channels)
        plane_block = jnp.roll(plane_block, (-sign * b, -sign * c), axis=(2, 3))
        pieces.append(plane_block)
    return jnp.concatenate(pieces, axis=4).reshape(-1, 27 * channels)


def with_neighbours(volume, cotangent):
    count = lax.axis_size("space")
    onward = [(i, (i + 1) % count) for i in range(count)]
    back = [((i + 1) % count, i) for i in range(count)]
    wide = cotangent.shape[3]
    packed = volume.reshape(1, 1, -1, wide)
    before = lax.ppermute(jnp.concatenate([packed, cotangent[:, 1:]], axis=2), "space", onward)
    after = lax.ppermute(jnp.concatenate([packed, cotangent[:, :1]], axis=2), "space", back)
    held = packed.shape[2]
    volumes = [before[:, :, :held].reshape(volume.shape), volume, after[:, :, :held].reshape(volume.shape)]
    cotangents = [before[:, :, held:], cotangent, after[:, :, held:]]
    return jnp.concatenate(volumes, axis=1), jnp.concatenate(cotangents, axis=1)


def summed_everywhere(local):
    devices = lax.axis_size(EVERY)
    rows, width = local.shape
    piece = 4 * ((rows + 4 * devices - 1) // (4 * devices))
    sent = jnp.pad(local.astype(jnp.bfloat16), ((0, piece * devices - rows), (0, 0)))
    terms = lax.all_to_all(sent.reshape(devices, piece, width), EVERY, 0, 0)
    total = jnp.sum(terms.astype(jnp.float32), axis=0).astype(jnp.bfloat16)
    spread = jnp.broadcast_to(total[None], (devices, piece, width))
    joined = lax.all_to_all(spread, EVERY, 0, 0)
    return joined.reshape(devices * piece, width)[:rows]


def per_device(volume, weight, cotangent, left_stat, right_stat):
    channels_in = weight.shape[0] // 27
    channels_out = weight.shape[1]
    leading, depth, height, wide = volume.shape
    across = wide // channels_in
    left_all = lax.all_gather(left_stat.astype(jnp.bfloat16), "dp", axis=0, tiled=True)
    volumes, cotangents = with_neighbours(volume, cotangent)
    patches = gather_patches(volumes, depth + 2, channels_in, 1)
    preact = jnp.dot(patches, weight, preferred_element_type=jnp.float32)
    sigmoid_val = jax.nn.sigmoid(preact)
    cells = (leading, depth + 2, height, across * channels_out)
    output = (preact * sigmoid_val).astype(jnp.bfloat16).reshape(cells)[:, 1:-1]
    upstream = cotangents.reshape(-1, channels_out).astype(jnp.float32)
    pre_grad = (upstream * sigmoid_val * (1.0 + preact * (1.0 - sigmoid_val))).astype(jnp.bfloat16)
    grad_padded = pre_grad.reshape(cells)
    plane = height * across
    local_grad = lax.dot_general(
        patches[plane:-plane],
        pre_grad[plane:-plane],
        (((0,), (0,)), ((), ())),
        preferred_element_type=jnp.float32,
    )
    voxels = leading * lax.axis_size("dp") * depth * lax.axis_size("space") * height * across
    rounded = summed_everywhere(local_grad / math.sqrt(voxels))
    gradient = rounded.astype(jnp.float32)
    back_patches = gather_patches(grad_padded, depth, channels_out, -1)
    flipped = (
        weight.reshape(27, channels_in, channels_out)
        .transpose(0, 2, 1)
        .reshape(27 * channels_out, channels_in)
    )
    input_grad = jnp.dot(back_patches, flipped, preferred_element_type=jnp.float32)
    input_grad = input_grad.astype(jnp.bfloat16).reshape(
        leading, depth, height, across * channels_in
    )
    row_count = left_stat.shape[0]
    fan_total = gradient.shape[0]
    first_row = lax.axis_index("dp") * row_count
    right_full = DECAY * right_stat + lax.dot_general(
        rounded, rounded, (((0,), (0,)), ((), ())), preferred_element_type=jnp.float32
    )
    right_root = small_root(right_full)
    carried = jnp.dot(gradient, right_root, precision=EXACT_MODE)
    left_full = DECAY * left_all.astype(jnp.float32) + lax.dot_general(
        rounded, rounded, (((1,), (1,)), ((), ())), preferred_element_type=jnp.float32
    )
    row_ids = lax.broadcasted_iota(jnp.int32, (fan_total, fan_total), 0)
    col_ids = lax.broadcasted_iota(jnp.int32, (fan_total, fan_total), 1)
    trace = jnp.sum(jnp.where(row_ids == col_ids, left_full, 0.0))
    scaled = (left_full / trace).astype(jnp.bfloat16)
    start = jnp.full((fan_total, 128), 1.0 / math.sqrt(fan_total), jnp.float32)
    block = jnp.concatenate([carried, start], axis=1)
    powers, lengths = [carried], []
    for degree in range(1, DEGREE + 1):
        block = jnp.dot(scaled, block.astype(jnp.bfloat16), preferred_element_type=jnp.float32)
        powers.append(block[:, :channels_out])
        lengths.append(jnp.sqrt(jnp.sum(block[:, channels_out] * block[:, channels_out])))
    share = lengths[POWER - 1] / lengths[POWER - 2]
    coeffs = root_coefficients()
    update = coeffs[0] * powers[0]
    factor = jnp.float32(1.0)
    for degree in range(1, DEGREE + 1):
        factor = factor / share
        update = update + (coeffs[degree] * factor) * powers[degree]
    update = update * (share * trace) ** (-0.25)
    update_norm = jnp.sqrt(jnp.sum(update * update))
    grad_norm = jnp.sqrt(jnp.sum(gradient * gradient))
    update_rows = lax.dynamic_slice_in_dim(update, first_row, row_count, 0)
    direction = update_rows * grad_norm / (update_norm + 1e-06)
    return (output, input_grad, gradient, direction)


def solution(mesh):
    placed = (P("dp", "space", None, None), P(), P("dp", "space", None, None), P("dp", None), P())
    return jax.shard_map(
        per_device,
        mesh=mesh,
        in_specs=placed,
        out_specs=(P("dp", "space", None, None), P("dp", "space", None, None), P(), P("dp", None)),
        check_vma=False,
    )
```

```python
import functools
import math

import jax
import jax.numpy as jnp
from jax import lax
from jax.experimental import pallas as pl
from jax.experimental.pallas import tpu as pltpu
from jax.sharding import PartitionSpec as P

POWER = 4
DEGREE = 6
DECAY = 0.9
EVERY = ("space", "dp")
VMEM = pl.BlockSpec(memory_space=pltpu.VMEM)
SMEM = pl.BlockSpec(memory_space=pltpu.SMEM)
BIG = pltpu.CompilerParams(vmem_limit_bytes=48 * 1024 * 1024)
ROWS_AT_ONCE = 432
CHUNKS = 4


def offset_list():
    return [(a, b, c) for a in (-1, 0, 1) for b in (-1, 0, 1) for c in (-1, 0, 1)]


def root_coefficients():
    terms_list = [(1, 5.0), (5, -5.0), (6, 4.0)]
    coeffs = [0.0] * 7
    for degree, factor in terms_list:
        for j in range(degree + 1):
            coeffs[j] += factor * math.comb(degree, j) * 1.25 ** (degree - j) * (-0.25) ** j / 4.0
    return coeffs


def rolled_rows(cells, shift):
    if shift == 0:
        return cells
    if shift > 0:
        return jnp.concatenate([cells[:, shift:], cells[:, :shift]], axis=1)
    height = cells.shape[1]
    return jnp.concatenate([cells[:, height + shift :], cells[:, : height + shift]], axis=1)


def conv_kernel(scale, before, volume, after, cotangent, weight, out, sent, pre_grad, patches):
    height = volume.shape[2]
    wide = volume.shape[3]
    lanes = weight.shape[1]
    half = lanes // 2
    across = wide // half
    depth = volume.shape[1]
    held = depth + 2
    rows = held * height
    cells = jnp.concatenate([before[0, :2], volume[0], after[0, :2]], axis=0).astype(jnp.float32)
    low = lax.broadcasted_iota(jnp.int32, (1, 1, lanes), 2) < half
    low_flat = lax.broadcasted_iota(jnp.int32, (1, lanes), 1) < half
    doubled = {}
    for pair in range(across // 2):
        both = cells[:, :, pair * lanes : (pair + 1) * lanes]
        turned = jnp.concatenate([both[:, :, half:], both[:, :, :half]], axis=2)
        for side, one in enumerate((jnp.where(low, both, turned), jnp.where(low, turned, both))):
            for b in (-1, 0, 1):
                moved = rolled_rows(one, b).astype(jnp.bfloat16)
                doubled[2 * pair + side, b] = moved.reshape((held + 2) * height, lanes)

    def piece(offset):
        a, b, c = offset
        first = (1 + a) * height
        return [doubled[(x + c) % across, b][first : first + rows] for x in range(across)]

    taps = [piece(o) for o in offset_list()]
    taps.append([jnp.zeros((rows, lanes), jnp.bfloat16)] * across)
    for j in range(len(taps) // 2):
        for x in range(across):
            patches[x * rows : (x + 1) * rows, j * lanes : (j + 1) * lanes] = jnp.where(
                low_flat, taps[2 * j][x], taps[2 * j + 1][x]
            )
    preact = jnp.dot(patches[...], weight[...], preferred_element_type=jnp.float32)
    sigmoid_val = jax.nn.sigmoid(preact)
    output = (preact * sigmoid_val).astype(jnp.bfloat16)
    inner = []
    upstream = []
    for x in range(across):
        span = slice(x * lanes, (x + 1) * lanes)
        place = (x % (across // 2)) * lanes
        side = 2 + x // (across // 2)
        upstream.append(before[0, side, :, place : place + lanes])
        upstream.extend(cotangent[0, p, :, span] for p in range(depth))
        upstream.append(after[0, side, :, place : place + lanes])
        for p in range(depth):
            first = x * rows + (1 + p) * height
            out[0, p, :, span] = output[first : first + height]
    upstream = jnp.concatenate(upstream, axis=0).astype(jnp.float32)
    slope = sigmoid_val * (1.0 + preact * (1.0 - sigmoid_val))
    grads = (upstream * slope).astype(jnp.bfloat16)
    pre_grad[...] = grads
    own = [slice(x * rows + height, x * rows + rows - height) for x in range(across)]
    own_patches = jnp.concatenate([patches[s, :] for s in own], axis=0)
    own_grads = jnp.concatenate([grads[s] for s in own], axis=0)
    local = lax.dot_general(
        own_patches, own_grads, (((0,), (0,)), ((), ())), preferred_element_type=jnp.float32
    )
    fan = patches.shape[1]
    sent[:fan, :] = (local * scale).astype(jnp.bfloat16)
    sent[fan:, :] = jnp.zeros((sent.shape[0] - fan, lanes), jnp.bfloat16)


def back_kernel(pre_grad, flipped, out, patches):
    height, depth = out.shape[2], out.shape[1]
    lanes = pre_grad.shape[1]
    across = out.shape[3] // (lanes // 2)
    rows = pre_grad.shape[0] // across
    held = rows // height
    own = depth * height
    grads = pre_grad[...].astype(jnp.float32).reshape(across, held, height, lanes)
    moved = {}
    for x in range(across):
        for b in (-1, 0, 1):
            moved[x, b] = rolled_rows(grads[x], -b).astype(jnp.bfloat16).reshape(rows, lanes)
    for k, (a, b, c) in enumerate(offset_list()):
        first = (1 - a) * height
        for x in range(across):
            patches[x * own : (x + 1) * own, k * lanes : (k + 1) * lanes] = moved[
                (x - c) % across, b
            ][first : first + own]
    result = jnp.dot(patches[...], flipped[...], preferred_element_type=jnp.float32)
    low = lax.broadcasted_iota(jnp.int32, (1, lanes), 1) < lanes // 2
    for pair in range(across // 2):
        left = result[2 * pair * own : (2 * pair + 1) * own]
        right = result[(2 * pair + 1) * own : (2 * pair + 2) * own]
        both = jnp.where(low, left, right).astype(jnp.bfloat16)
        for p in range(depth):
            out[0, p, :, pair * lanes : (pair + 1) * lanes] = both[p * height : (p + 1) * height]


def whole_sum(values):
    return jnp.sum(jnp.sum(values, axis=0, keepdims=True), axis=1, keepdims=True)


def diagonal_sum(block):
    row_ids = lax.broadcasted_iota(jnp.int32, block.shape, 0)
    col_ids = lax.broadcasted_iota(jnp.int32, block.shape, 1)
    return whole_sum(jnp.where(row_ids == col_ids, block, 0.0))


def sharp_dot(left, right):
    return jnp.dot(
        left, right, precision=lax.Precision.HIGHEST, preferred_element_type=jnp.float32
    )


def right_root_of(full, coeffs):
    size = full.shape[0]
    trace = diagonal_sum(full)
    scaled = full / trace
    vector = jnp.full((1, size), 1.0 / math.sqrt(size), jnp.float32)
    lengths = []
    for step in range(POWER):
        vector = jnp.sum(scaled * vector, axis=1 - step % 2, keepdims=True)
        lengths.append(jnp.sqrt(whole_sum(vector * vector)))
    largest = trace * lengths[POWER - 1] / lengths[POWER - 2]
    unit = full / largest
    row_ids = lax.broadcasted_iota(jnp.int32, full.shape, 0)
    col_ids = lax.broadcasted_iota(jnp.int32, full.shape, 1)
    identity = (row_ids == col_ids).astype(jnp.float32)
    square = sharp_dot(unit, unit)
    cube = sharp_dot(square, unit)
    low = coeffs[0] * identity + coeffs[1] * unit + coeffs[2] * square + coeffs[3] * cube
    high = coeffs[4] * unit + coeffs[5] * square + coeffs[6] * cube
    return (low + sharp_dot(cube, high)) * lax.rsqrt(jnp.sqrt(largest))


def refresh_kernel(first, joined, left_far, right_stat, gradient, direction, left, block, powers, sems):
    fan, width = gradient.shape
    part = fan // CHUNKS
    copies = []
    for k in range(CHUNKS):
        rows = pl.ds(k * part, part)
        copies.append(pltpu.make_async_copy(left_far.at[rows], left.at[rows], sems.at[k]))
        copies[-1].start()
    coeffs = root_coefficients()
    rounded = joined[:fan, :]
    wide_grad = rounded.astype(jnp.float32)
    gradient[...] = wide_grad
    grad_square = whole_sum(wide_grad * wide_grad)
    right_full = DECAY * right_stat[...] + lax.dot_general(
        rounded, rounded, (((0,), (0,)), ((), ())), preferred_element_type=jnp.float32
    )
    root = right_root_of(right_full, coeffs)
    root_high = root.astype(jnp.bfloat16)
    root_low = (root - root_high.astype(jnp.float32)).astype(jnp.bfloat16)
    parts = jnp.dot(
        rounded,
        jnp.concatenate([root_high, root_low], axis=1),
        preferred_element_type=jnp.float32,
    )
    carried = parts[:, :width] + parts[:, width:]
    powers[0] = carried
    block[0, :, :width] = carried.astype(jnp.bfloat16)
    block[0, :, width:] = jnp.full((fan, width), 1.0 / math.sqrt(fan), jnp.bfloat16)
    for copy in copies:
        copy.wait()
    trace = grad_square
    for start in range(0, fan, width):
        size = min(width, fan - start)
        trace = trace + DECAY * diagonal_sum(
            left[start : start + size, start : start + size].astype(jnp.float32)
        )
    inverse = 1.0 / trace

    def add_gradient(k, _):
        rows = pl.ds(pl.multiple_of(k * 144, 144), 144)
        outer = lax.dot_general(
            joined[rows, :], rounded, (((1,), (1,)), ((), ())), preferred_element_type=jnp.float32
        )
        left[rows, :] = (DECAY * left[rows, :].astype(jnp.float32) + outer).astype(jnp.bfloat16)
        return 0

    lax.fori_loop(0, fan // 144, add_gradient, 0)
    squares = {}
    for degree in range(1, DEGREE + 1):
        held = block[(degree - 1) % 2]

        def multiply(k, square, held=held, degree=degree):
            rows = pl.ds(pl.multiple_of(k * ROWS_AT_ONCE, ROWS_AT_ONCE), ROWS_AT_ONCE)
            product = inverse * jnp.dot(left[rows, :], held, preferred_element_type=jnp.float32)
            powers[degree, rows, :] = product[:, :width]
            if degree < DEGREE:
                block[degree % 2, rows, :] = product.astype(jnp.bfloat16)
            if degree in (POWER - 1, POWER):
                column = product[:, width:]
                square = square + jnp.sum(column * column, axis=0, keepdims=True)
            return square

        squares[degree] = lax.fori_loop(
            0, fan // ROWS_AT_ONCE, multiply, jnp.zeros((1, width), jnp.float32)
        )
    share = jnp.sqrt(squares[POWER][:, :1]) / jnp.sqrt(squares[POWER - 1][:, :1])
    update = coeffs[0] * powers[0]
    factor = 1.0 / share
    scale = factor
    for degree in range(1, DEGREE + 1):
        update = update + (coeffs[degree] * scale) * powers[degree]
        scale = scale * factor
    update = update * lax.rsqrt(jnp.sqrt(share * trace))
    powers[0] = update
    update_norm = jnp.sqrt(whole_sum(update * update))
    ratio = jnp.sqrt(grad_square) / (update_norm + 1e-06)
    size = direction.shape[0]
    direction[...] = powers[0, pl.ds(pl.multiple_of(first[0], 8), size), :] * ratio


def convolved(before, volume, after, cotangent, weight, scale, spread_rows):
    leading, depth, height, wide = volume.shape
    lanes = weight.shape[1]
    cells = wide // (lanes // 2) * (depth + 2) * height
    return pl.pallas_call(
        functools.partial(conv_kernel, scale),
        out_shape=(
            jax.ShapeDtypeStruct(cotangent.shape, jnp.bfloat16),
            jax.ShapeDtypeStruct((spread_rows, lanes), jnp.bfloat16),
            jax.ShapeDtypeStruct((cells, lanes), jnp.bfloat16),
        ),
        in_specs=[VMEM] * 5,
        out_specs=(VMEM,) * 3,
        scratch_shapes=[pltpu.VMEM((cells, weight.shape[0]), jnp.bfloat16)],
        compiler_params=BIG,
        name="conv",
    )(before, volume, after, cotangent, weight)


def convolved_back(pre_grad, flipped, volume):
    leading, depth, height, wide = volume.shape
    lanes = pre_grad.shape[1]
    own = wide // (lanes // 2) * depth * height
    return pl.pallas_call(
        back_kernel,
        out_shape=jax.ShapeDtypeStruct(volume.shape, jnp.bfloat16),
        in_specs=[VMEM] * 2,
        out_specs=VMEM,
        scratch_shapes=[pltpu.VMEM((own, flipped.shape[0]), jnp.bfloat16)],
        compiler_params=BIG,
        cost_estimate=pl.CostEstimate(
            flops=2 * own * flipped.size, bytes_accessed=2 * own * flipped.shape[0], transcendentals=0
        ),
        name="conv_back",
    )(pre_grad, flipped)


def refreshed(first_row, joined, left_all, right_stat, fan, row_count):
    width = right_stat.shape[0]
    return pl.pallas_call(
        refresh_kernel,
        out_shape=(
            jax.ShapeDtypeStruct((fan, width), jnp.float32),
            jax.ShapeDtypeStruct((row_count, width), jnp.float32),
        ),
        in_specs=[SMEM, VMEM, pl.BlockSpec(memory_space=pl.ANY), VMEM],
        out_specs=(VMEM, VMEM),
        scratch_shapes=[
            pltpu.VMEM((fan, fan), jnp.bfloat16),
            pltpu.VMEM((2, fan, 2 * width), jnp.bfloat16),
            pltpu.VMEM((DEGREE + 1, fan, width), jnp.float32),
            pltpu.SemaphoreType.DMA((CHUNKS,)),
        ],
        compiler_params=BIG,
        name="refresh",
    )(first_row, joined, left_all, right_stat)


def per_device(volume, weight, cotangent, left_stat, right_stat):
    fan, lanes = weight.shape
    leading, depth, height, wide = volume.shape
    devices = lax.axis_size(EVERY)
    slabs = lax.axis_size("space")
    left_all = lax.all_gather(left_stat.astype(jnp.bfloat16), "dp", axis=0, tiled=True)
    onward = [(i, (i + 1) % slabs) for i in range(slabs)]
    back = [((i + 1) % slabs, i) for i in range(slabs)]

    def with_plane(plane):
        return jnp.concatenate([volume, plane[..., :wide], plane[..., wide:]], axis=1)

    before = lax.ppermute(with_plane(cotangent[:, -1:]), "space", onward)
    after = lax.ppermute(with_plane(cotangent[:, :1]), "space", back)
    channels = fan // 27
    flipped = weight.reshape(27, channels, lanes).transpose(0, 2, 1).reshape(27 * lanes, channels)
    flipped = jnp.concatenate([flipped, flipped], axis=1)
    padded_fan = (fan + lanes - 1) // lanes * lanes
    padded = jnp.pad(weight, ((0, padded_fan - fan), (0, 0)))
    piece = 4 * ((fan + 4 * devices - 1) // (4 * devices))
    cells = slabs * lax.axis_size("dp") * leading * depth * height * (wide // channels)
    output, sent, pre_grad = convolved(
        before, volume, after, cotangent, padded, 1.0 / math.sqrt(cells), piece * devices
    )
    terms = lax.all_to_all(sent.reshape(devices, piece, lanes), EVERY, 0, 0)
    total = jnp.sum(terms.astype(jnp.float32), axis=0).astype(jnp.bfloat16)
    joined = lax.all_to_all(jnp.broadcast_to(total[None], terms.shape), EVERY, 0, 0)
    input_grad = convolved_back(pre_grad, flipped, volume)
    row_count = left_stat.shape[0]
    first_row = (lax.axis_index("dp") * row_count).astype(jnp.int32).reshape(1)
    gradient, direction = refreshed(
        first_row, joined.reshape(devices * piece, lanes), left_all, right_stat, fan, row_count
    )
    return output, input_grad, gradient, direction


def solution(mesh):
    placed = (P("dp", "space", None, None), P(), P("dp", "space", None, None), P("dp", None), P())
    return jax.shard_map(
        per_device,
        mesh=mesh,
        in_specs=placed,
        out_specs=(P("dp", "space", None, None), P("dp", "space", None, None), P(), P("dp", None)),
        check_vma=False,
    )
```

```python
import functools
import math

import jax
import jax.numpy as jnp
from jax import lax
from jax.experimental import pallas as pl
from jax.experimental.pallas import tpu as pltpu
from jax.sharding import Mesh
from jax.sharding import PartitionSpec as P

POWER = 4
DEGREE = 6
DECAY = 0.9
VMEM = pl.BlockSpec(memory_space=pltpu.VMEM)
SMEM = pl.BlockSpec(memory_space=pltpu.SMEM)
BIG = pltpu.CompilerParams(vmem_limit_bytes=48 * 1024 * 1024)


def offset_list():
    return [(a, b, c) for a in (-1, 0, 1) for b in (-1, 0, 1) for c in (-1, 0, 1)]


def root_coefficients():
    terms_list = [(1, 5.0), (5, -5.0), (6, 4.0)]
    coeffs = [0.0] * 7
    for degree, factor in terms_list:
        for j in range(degree + 1):
            coeffs[j] += factor * math.comb(degree, j) * 1.25 ** (degree - j) * (-0.25) ** j / 4.0
    return coeffs


def rolled_rows(cells, shift):
    if shift == 0:
        return cells
    if shift > 0:
        return jnp.concatenate([cells[:, shift:], cells[:, :shift]], axis=1)
    height = cells.shape[1]
    return jnp.concatenate([cells[:, height + shift :], cells[:, : height + shift]], axis=1)


def conv_kernel(
    scale, place, before, volume, after, cotangent, weight, out, keep, give, pre_grad, patches
):
    height = volume.shape[2]
    wide = volume.shape[3]
    lanes = weight.shape[1]
    half = lanes // 2
    across = wide // half
    depth = volume.shape[1]
    held = depth + 2
    rows = held * height
    cells = jnp.concatenate([before[0, :2], volume[0], after[0, :2]], axis=0).astype(jnp.float32)
    low = lax.broadcasted_iota(jnp.int32, (1, 1, lanes), 2) < half
    low_flat = lax.broadcasted_iota(jnp.int32, (1, lanes), 1) < half
    doubled = {}
    for pair in range(across // 2):
        both = cells[:, :, pair * lanes : (pair + 1) * lanes]
        turned = jnp.concatenate([both[:, :, half:], both[:, :, :half]], axis=2)
        for side, one in enumerate((jnp.where(low, both, turned), jnp.where(low, turned, both))):
            for b in (-1, 0, 1):
                moved = rolled_rows(one, b).astype(jnp.bfloat16)
                doubled[2 * pair + side, b] = moved.reshape((held + 2) * height, lanes)

    def piece(offset):
        a, b, c = offset
        first = (1 + a) * height
        return [doubled[(x + c) % across, b][first : first + rows] for x in range(across)]

    taps = [piece(o) for o in offset_list()]
    taps.append([jnp.zeros((rows, lanes), jnp.bfloat16)] * across)
    for j in range(len(taps) // 2):
        for x in range(across):
            patches[x * rows : (x + 1) * rows, j * lanes : (j + 1) * lanes] = jnp.where(
                low_flat, taps[2 * j][x], taps[2 * j + 1][x]
            )
    preact = jnp.dot(patches[...], weight[...], preferred_element_type=jnp.float32)
    sigmoid_val = jax.nn.sigmoid(preact)
    output = (preact * sigmoid_val).astype(jnp.bfloat16)
    inner = []
    upstream = []
    for x in range(across):
        span = slice(x * lanes, (x + 1) * lanes)
        begin = (x % (across // 2)) * lanes
        side = 2 + x // (across // 2)
        upstream.append(before[0, side, :, begin : begin + lanes])
        upstream.extend(cotangent[0, p, :, span] for p in range(depth))
        upstream.append(after[0, side, :, begin : begin + lanes])
        for p in range(depth):
            first = x * rows + (1 + p) * height
            out[0, p, :, span] = output[first : first + height]
    upstream = jnp.concatenate(upstream, axis=0).astype(jnp.float32)
    slope = sigmoid_val * (1.0 + preact * (1.0 - sigmoid_val))
    grads = (upstream * slope).astype(jnp.bfloat16)
    pre_grad[...] = grads
    own = [slice(x * rows + height, x * rows + rows - height) for x in range(across)]
    own_patches = jnp.concatenate([patches[s, :] for s in own], axis=0)
    own_grads = jnp.concatenate([grads[s] for s in own], axis=0)
    local = lax.dot_general(
        own_patches, own_grads, (((0,), (0,)), ((), ())), preferred_element_type=jnp.float32
    )
    local = local * scale
    part = keep.shape[0]
    rest = jnp.zeros((2 * part - local.shape[0], lanes), jnp.float32)
    head, tail = local[:part], jnp.concatenate([local[part:], rest], axis=0)
    leading = place[0] == 0
    keep[...] = jnp.where(leading, head, tail)
    give[...] = jnp.where(leading, tail, head).astype(jnp.bfloat16)


def back_kernel(pre_grad, flipped, out, patches):
    height, depth = out.shape[2], out.shape[1]
    lanes = pre_grad.shape[1]
    across = out.shape[3] // (lanes // 2)
    rows = pre_grad.shape[0] // across
    held = rows // height
    own = depth * height
    grads = pre_grad[...].astype(jnp.float32).reshape(across, held, height, lanes)
    moved = {}
    for x in range(across):
        for b in (-1, 0, 1):
            moved[x, b] = rolled_rows(grads[x], -b).astype(jnp.bfloat16).reshape(rows, lanes)
    for k, (a, b, c) in enumerate(offset_list()):
        first = (1 - a) * height
        for x in range(across):
            patches[x * own : (x + 1) * own, k * lanes : (k + 1) * lanes] = moved[
                (x - c) % across, b
            ][first : first + own]
    result = jnp.dot(patches[...], flipped[...], preferred_element_type=jnp.float32)
    low = lax.broadcasted_iota(jnp.int32, (1, lanes), 1) < lanes // 2
    for pair in range(across // 2):
        left = result[2 * pair * own : (2 * pair + 1) * own]
        right = result[(2 * pair + 1) * own : (2 * pair + 2) * own]
        both = jnp.where(low, left, right).astype(jnp.bfloat16)
        for p in range(depth):
            out[0, p, :, pair * lanes : (pair + 1) * lanes] = both[p * height : (p + 1) * height]


def whole_sum(values):
    return jnp.sum(jnp.sum(values, axis=0, keepdims=True), axis=1, keepdims=True)


def diagonal_sum(block):
    row_ids = lax.broadcasted_iota(jnp.int32, block.shape, 0)
    col_ids = lax.broadcasted_iota(jnp.int32, block.shape, 1)
    return whole_sum(jnp.where(row_ids == col_ids, block, 0.0))


def sharp_dot(left, right):
    return jnp.dot(
        left, right, precision=lax.Precision.HIGHEST, preferred_element_type=jnp.float32
    )


def right_root_of(full, coeffs):
    size = full.shape[0]
    trace = diagonal_sum(full)
    scaled = full / trace
    vector = jnp.full((1, size), 1.0 / math.sqrt(size), jnp.float32)
    lengths = []
    for step in range(POWER):
        vector = jnp.sum(scaled * vector, axis=1 - step % 2, keepdims=True)
        lengths.append(jnp.sqrt(whole_sum(vector * vector)))
    largest = trace * lengths[POWER - 1] / lengths[POWER - 2]
    unit = full / largest
    row_ids = lax.broadcasted_iota(jnp.int32, full.shape, 0)
    col_ids = lax.broadcasted_iota(jnp.int32, full.shape, 1)
    identity = (row_ids == col_ids).astype(jnp.float32)
    square = sharp_dot(unit, unit)
    cube = sharp_dot(square, unit)
    low = coeffs[0] * identity + coeffs[1] * unit + coeffs[2] * square + coeffs[3] * cube
    high = coeffs[4] * unit + coeffs[5] * square + coeffs[6] * cube
    return (low + sharp_dot(cube, high)) * lax.rsqrt(jnp.sqrt(largest))


def pack_kernel(rows, packed):
    count, fan = rows.shape
    spare = packed.shape[0] - count
    gap = jnp.zeros((count, spare), jnp.float32)
    pieces = []
    for start in range(0, fan, count):
        pieces.extend([rows[:, start : start + count], gap])
    wide = jnp.concatenate(pieces, axis=1)
    tall = jnp.concatenate([wide, jnp.zeros((spare, wide.shape[1]), jnp.float32)], axis=0)
    packed[...] = tall.astype(jnp.bfloat16)


def refresh_kernel(
    place, mine, theirs, left_mine, left_theirs, right_stat, gradient, direction,
    left, spaced, tall_ref, block, powers, window,
):
    fan, width = gradient.shape
    count = direction.shape[0]
    blocks = fan // count
    step = left.shape[0] // blocks
    core = place[0]
    coeffs = root_coefficients()
    own, other = mine[...].astype(jnp.float32), theirs[...].astype(jnp.float32)
    half = own.shape[0]
    gradient[:half, :] = jnp.where(core == 0, own, other)
    gradient[half:, :] = jnp.where(core == 0, other, own)[: fan - half]
    grad_square = whole_sum(gradient[...] * gradient[...])
    for k in range(blocks):
        spaced[k * step : k * step + count, :] = gradient[k * count : (k + 1) * count, :]
        spaced[k * step + count : (k + 1) * step, :] = jnp.zeros((step - count, width), jnp.float32)
    tall = spaced[...].astype(jnp.bfloat16)
    tall_ref[...] = tall
    flat = jnp.transpose(spaced[...]).astype(jnp.bfloat16)
    for source, side in ((left_mine, core), (left_theirs, 1 - core)):

        def add_gradient(chip, _, source=source, side=side):
            rows = pl.ds(pl.multiple_of((2 * chip + side) * step, step), step)
            outer = jnp.dot(tall_ref[rows, :], flat, preferred_element_type=jnp.float32)
            held = source[pl.ds(pl.multiple_of(chip * step, step), step), :].astype(jnp.float32)
            left[rows, :] = (DECAY * held + outer).astype(jnp.bfloat16)
            return 0

        lax.fori_loop(0, blocks // 2, add_gradient, 0)
    trace = jnp.zeros((1, 1), jnp.float32)
    for start in range(0, left.shape[0], width):
        square = left[start : start + width, start : start + width]
        trace = trace + diagonal_sum(square.astype(jnp.float32))
    inverse = 1.0 / trace
    right_full = DECAY * right_stat[...] + jnp.dot(flat, tall, preferred_element_type=jnp.float32)
    root = right_root_of(right_full, coeffs)
    root_high = root.astype(jnp.bfloat16)
    root_low = (root - root_high.astype(jnp.float32)).astype(jnp.bfloat16)
    parts = jnp.dot(
        jnp.concatenate([root_high, root_low], axis=0), flat, preferred_element_type=jnp.float32
    )
    carried = parts[:width] + parts[width:]
    powers[0] = carried
    vectors = block.shape[1] - width
    first_row = lax.broadcasted_iota(jnp.int32, (vectors, left.shape[0]), 0) == 0
    block[0, :width, :] = carried.astype(jnp.bfloat16)
    block[0, width:, :] = jnp.where(first_row, 1.0 / math.sqrt(fan), 0.0).astype(jnp.bfloat16)
    squares = {}
    for degree in range(1, DEGREE + 1):
        product = inverse * jnp.dot(
            block[(degree - 1) % 2], left[...], preferred_element_type=jnp.float32
        )
        powers[degree] = product[:width]
        if degree < DEGREE:
            block[degree % 2] = product.astype(jnp.bfloat16)
        if degree in (POWER - 1, POWER):
            squares[degree] = whole_sum(product[width:] * product[width:])
    share = jnp.sqrt(squares[POWER]) / jnp.sqrt(squares[POWER - 1])
    update = coeffs[0] * powers[0]
    factor = 1.0 / share
    scale = factor
    for degree in range(1, DEGREE + 1):
        update = update + (coeffs[degree] * scale) * powers[degree]
        scale = scale * factor
    update = update * lax.rsqrt(jnp.sqrt(share * trace))
    powers[0] = update
    update_norm = jnp.sqrt(whole_sum(update * update))
    ratio = jnp.sqrt(grad_square) / (update_norm + 1e-06)
    span = window.shape[0]
    first = place[1] * step
    base = jnp.minimum(first // width * width, left.shape[0] - span)
    window[...] = jnp.transpose(powers[0, :, pl.ds(pl.multiple_of(base, width), span)])
    direction[...] = window[pl.ds(pl.multiple_of(first - base, 8), count), :] * ratio


def convolved(place, before, volume, after, cotangent, weight, scale, part):
    leading, depth, height, wide = volume.shape
    lanes = weight.shape[1]
    cells = wide // (lanes // 2) * (depth + 2) * height
    return pl.pallas_call(
        functools.partial(conv_kernel, scale),
        out_shape=(
            jax.ShapeDtypeStruct(cotangent.shape, jnp.bfloat16),
            jax.ShapeDtypeStruct((part, lanes), jnp.float32),
            jax.ShapeDtypeStruct((part, lanes), jnp.bfloat16),
            jax.ShapeDtypeStruct((cells, lanes), jnp.bfloat16),
        ),
        in_specs=[SMEM] + [VMEM] * 5,
        out_specs=(VMEM,) * 4,
        scratch_shapes=[pltpu.VMEM((cells, weight.shape[0]), jnp.bfloat16)],
        compiler_params=BIG,
        name="conv",
    )(place, before, volume, after, cotangent, weight)


def convolved_back(pre_grad, flipped, volume):
    leading, depth, height, wide = volume.shape
    lanes = pre_grad.shape[1]
    own = wide // (lanes // 2) * depth * height
    return pl.pallas_call(
        back_kernel,
        out_shape=jax.ShapeDtypeStruct(volume.shape, jnp.bfloat16),
        in_specs=[VMEM] * 2,
        out_specs=VMEM,
        scratch_shapes=[pltpu.VMEM((own, flipped.shape[0]), jnp.bfloat16)],
        compiler_params=BIG,
        cost_estimate=pl.CostEstimate(
            flops=2 * own * flipped.size, bytes_accessed=2 * own * flipped.shape[0], transcendentals=0
        ),
        name="conv_back",
    )(pre_grad, flipped)


def add_kernel(keep, got, passing, sent, passed):
    sent[...] = (keep[...] + got[...].astype(jnp.float32)).astype(jnp.bfloat16)


def added(keep, got, passing):
    far = pl.BlockSpec(memory_space=pl.ANY)
    return pl.pallas_call(
        add_kernel,
        out_shape=(
            jax.ShapeDtypeStruct(got.shape, jnp.bfloat16),
            jax.ShapeDtypeStruct(passing.shape, passing.dtype),
        ),
        in_specs=[VMEM, VMEM, far],
        out_specs=(VMEM, far),
        input_output_aliases={2: 1},
        name="add",
    )(keep, got, passing)


def packed_rows(rows):
    count, fan = rows.shape
    step = (count + 31) // 32 * 32
    return pl.pallas_call(
        pack_kernel,
        out_shape=jax.ShapeDtypeStruct((step, fan // count * step), jnp.bfloat16),
        in_specs=[VMEM],
        out_specs=VMEM,
        compiler_params=BIG,
        name="pack",
    )(rows)


def refreshed(place, mine, theirs, left_mine, left_theirs, right_stat, fan, count):
    width = right_stat.shape[0]
    size = left_mine.shape[1]
    return pl.pallas_call(
        refresh_kernel,
        out_shape=(
            jax.ShapeDtypeStruct((fan, width), jnp.float32),
            jax.ShapeDtypeStruct((count, width), jnp.float32),
        ),
        in_specs=[SMEM] + [VMEM] * 5,
        out_specs=(VMEM, VMEM),
        scratch_shapes=[
            pltpu.VMEM((size, size), jnp.bfloat16),
            pltpu.VMEM((size, width), jnp.float32),
            pltpu.VMEM((size, width), jnp.bfloat16),
            pltpu.VMEM((2, width + 16, size), jnp.bfloat16),
            pltpu.VMEM((DEGREE + 1, width, size), jnp.float32),
            pltpu.VMEM((3 * width, width), jnp.float32),
        ],
        compiler_params=BIG,
        name="refresh",
    )(place, mine, theirs, left_mine, left_theirs, right_stat)


def per_device(volume, weight, cotangent, left_stat, right_stat):
    fan, lanes = weight.shape
    leading, depth, height, wide = volume.shape
    slabs = lax.axis_size("space")
    chips = lax.axis_size(("space", "chip"))
    swap = [(0, 1), (1, 0)]
    core = lax.axis_index("core")
    place = jnp.stack([core, lax.axis_index(("chip", "core"))]).astype(jnp.int32)
    onward = [(i, (i + 1) % slabs) for i in range(slabs)]
    back = [((i + 1) % slabs, i) for i in range(slabs)]

    def with_plane(plane):
        return jnp.concatenate([volume, plane[..., :wide], plane[..., wide:]], axis=1)

    before = lax.ppermute(with_plane(cotangent[:, -1:]), "space", onward)
    after = lax.ppermute(with_plane(cotangent[:, :1]), "space", back)
    left_mine = lax.all_gather(packed_rows(left_stat), "chip", axis=0, tiled=True)
    channels = fan // 27
    flipped = weight.reshape(27, channels, lanes).transpose(0, 2, 1).reshape(27 * lanes, channels)
    flipped = jnp.concatenate([flipped, flipped], axis=1)
    padded_fan = (fan + lanes - 1) // lanes * lanes
    padded = jnp.pad(weight, ((0, padded_fan - fan), (0, 0)))
    piece = 4 * ((fan + 8 * chips - 1) // (8 * chips))
    cells = slabs * lax.axis_size(("chip", "core")) * leading * depth * height * (wide // channels)
    output, keep, give, pre_grad = convolved(
        place, before, volume, after, cotangent, padded, 1.0 / math.sqrt(cells), piece * chips
    )
    got = lax.ppermute(give, "core", swap)
    sent, left_mine = added(keep, got, left_mine)
    left_theirs = lax.ppermute(left_mine, "core", swap)
    terms = lax.all_to_all(sent.reshape(chips, piece, lanes), ("space", "chip"), 0, 0)
    total = jnp.sum(terms.astype(jnp.float32), axis=0).astype(jnp.bfloat16)
    spread = jnp.broadcast_to(total[None], terms.shape)
    mine = lax.all_to_all(spread, ("space", "chip"), 0, 0).reshape(chips * piece, lanes)
    theirs = lax.ppermute(mine, "core", swap)
    input_grad = convolved_back(pre_grad, flipped, volume)
    gradient, direction = refreshed(
        place, mine, theirs, left_mine, left_theirs, right_stat, fan, left_stat.shape[0]
    )
    return output, input_grad, gradient, direction


def solution(mesh):
    cut = Mesh(mesh.devices.reshape(mesh.shape["space"], -1, 2), ("space", "chip", "core"))
    parts = ("chip", "core")
    slab = P(parts, "space", None, None)
    return jax.shard_map(
        per_device,
        mesh=cut,
        in_specs=(slab, P(), slab, P(parts, None), P()),
        out_specs=(slab, slab, P(), P(parts, None)),
        check_vma=False,
    )
```

```python
import functools
import math

import jax
import jax.numpy as jnp
from jax import lax
from jax.experimental import pallas as pl
from jax.experimental.pallas import tpu as pltpu
from jax.sharding import Mesh
from jax.sharding import PartitionSpec as P

POWER = 4
DEGREE = 6
DECAY = 0.9
VMEM = pl.BlockSpec(memory_space=pltpu.VMEM)
SMEM = pl.BlockSpec(memory_space=pltpu.SMEM)


def room(mebibytes):
    return pltpu.CompilerParams(vmem_limit_bytes=mebibytes * 1024 * 1024)


def offset_list():
    return [(a, b, c) for a in (-1, 0, 1) for b in (-1, 0, 1) for c in (-1, 0, 1)]


def root_coefficients():
    terms_list = [(1, 5.0), (5, -5.0), (6, 4.0)]
    coeffs = [0.0] * 7
    for degree, factor in terms_list:
        for j in range(degree + 1):
            coeffs[j] += factor * math.comb(degree, j) * 1.25 ** (degree - j) * (-0.25) ** j / 4.0
    return coeffs


def rolled_rows(cells, shift):
    if shift == 0:
        return cells
    if shift > 0:
        return jnp.concatenate([cells[:, shift:], cells[:, :shift]], axis=1)
    height = cells.shape[1]
    return jnp.concatenate([cells[:, height + shift :], cells[:, : height + shift]], axis=1)


def conv_kernel(
    scale, place, before, volume, after, cotangent, weight, out, keep, give, pre_grad, patches
):
    height = volume.shape[2]
    wide = volume.shape[3]
    lanes = weight.shape[1]
    half = lanes // 2
    across = wide // half
    depth = volume.shape[1]
    held = depth + 2
    rows = held * height
    cells = jnp.concatenate([before[0, :2], volume[0], after[0, :2]], axis=0).astype(jnp.float32)
    low = lax.broadcasted_iota(jnp.int32, (1, 1, lanes), 2) < half
    low_flat = lax.broadcasted_iota(jnp.int32, (1, lanes), 1) < half
    doubled = {}
    for pair in range(across // 2):
        both = cells[:, :, pair * lanes : (pair + 1) * lanes]
        turned = jnp.concatenate([both[:, :, half:], both[:, :, :half]], axis=2)
        for side, one in enumerate((jnp.where(low, both, turned), jnp.where(low, turned, both))):
            for b in (-1, 0, 1):
                moved = rolled_rows(one, b).astype(jnp.bfloat16)
                doubled[2 * pair + side, b] = moved.reshape((held + 2) * height, lanes)

    def piece(offset):
        a, b, c = offset
        first = (1 + a) * height
        return [doubled[(x + c) % across, b][first : first + rows] for x in range(across)]

    taps = [piece(o) for o in offset_list()]
    taps.append([jnp.zeros((rows, lanes), jnp.bfloat16)] * across)
    for j in range(len(taps) // 2):
        for x in range(across):
            patches[x * rows : (x + 1) * rows, j * lanes : (j + 1) * lanes] = jnp.where(
                low_flat, taps[2 * j][x], taps[2 * j + 1][x]
            )
    preact = jnp.dot(patches[...], weight[...], preferred_element_type=jnp.float32)
    sigmoid_val = jax.nn.sigmoid(preact)
    output = (preact * sigmoid_val).astype(jnp.bfloat16)
    inner = []
    upstream = []
    for x in range(across):
        span = slice(x * lanes, (x + 1) * lanes)
        begin = (x % (across // 2)) * lanes
        side = 2 + x // (across // 2)
        upstream.append(before[0, side, :, begin : begin + lanes])
        upstream.extend(cotangent[0, p, :, span] for p in range(depth))
        upstream.append(after[0, side, :, begin : begin + lanes])
        for p in range(depth):
            first = x * rows + (1 + p) * height
            out[0, p, :, span] = output[first : first + height]
    upstream = jnp.concatenate(upstream, axis=0).astype(jnp.float32)
    slope = sigmoid_val * (1.0 + preact * (1.0 - sigmoid_val))
    grads = (upstream * slope).astype(jnp.bfloat16)
    pre_grad[...] = grads
    own = [slice(x * rows + height, x * rows + rows - height) for x in range(across)]
    own_patches = jnp.concatenate([patches[s, :] for s in own], axis=0)
    own_grads = jnp.concatenate([grads[s] for s in own], axis=0)
    local = lax.dot_general(
        own_patches, own_grads, (((0,), (0,)), ((), ())), preferred_element_type=jnp.float32
    )
    local = local * scale
    part = keep.shape[0]
    rest = jnp.zeros((2 * part - local.shape[0], lanes), jnp.float32)
    head, tail = local[:part], jnp.concatenate([local[part:], rest], axis=0)
    leading = place[0] == 0
    keep[...] = jnp.where(leading, head, tail)
    give[...] = jnp.where(leading, tail, head).astype(jnp.bfloat16)


def back_kernel(pre_grad, flipped, out, patches):
    height, depth = out.shape[2], out.shape[1]
    lanes = pre_grad.shape[1]
    across = out.shape[3] // (lanes // 2)
    rows = pre_grad.shape[0] // across
    held = rows // height
    own = depth * height
    grads = pre_grad[...].astype(jnp.float32).reshape(across, held, height, lanes)
    moved = {}
    for x in range(across):
        for b in (-1, 0, 1):
            moved[x, b] = rolled_rows(grads[x], -b).astype(jnp.bfloat16).reshape(rows, lanes)
    for k, (a, b, c) in enumerate(offset_list()):
        first = (1 - a) * height
        for x in range(across):
            patches[x * own : (x + 1) * own, k * lanes : (k + 1) * lanes] = moved[
                (x - c) % across, b
            ][first : first + own]
    result = jnp.dot(patches[...], flipped[...], preferred_element_type=jnp.float32)
    low = lax.broadcasted_iota(jnp.int32, (1, lanes), 1) < lanes // 2
    for pair in range(across // 2):
        left = result[2 * pair * own : (2 * pair + 1) * own]
        right = result[(2 * pair + 1) * own : (2 * pair + 2) * own]
        both = jnp.where(low, left, right).astype(jnp.bfloat16)
        for p in range(depth):
            out[0, p, :, pair * lanes : (pair + 1) * lanes] = both[p * height : (p + 1) * height]


def whole_sum(values):
    return jnp.sum(jnp.sum(values, axis=0, keepdims=True), axis=1, keepdims=True)


def diagonal_sum(block):
    row_ids = lax.broadcasted_iota(jnp.int32, block.shape, 0)
    col_ids = lax.broadcasted_iota(jnp.int32, block.shape, 1)
    return whole_sum(jnp.where(row_ids == col_ids, block, 0.0))


def sharp_dot(left, right):
    return jnp.dot(
        left, right, precision=lax.Precision.HIGHEST, preferred_element_type=jnp.float32
    )


def right_root_of(full, coeffs):
    size = full.shape[0]
    trace = diagonal_sum(full)
    scaled = full / trace
    vector = jnp.full((1, size), 1.0 / math.sqrt(size), jnp.float32)
    lengths = []
    for step in range(POWER):
        vector = jnp.sum(scaled * vector, axis=1 - step % 2, keepdims=True)
        lengths.append(jnp.sqrt(whole_sum(vector * vector)))
    largest = trace * lengths[POWER - 1] / lengths[POWER - 2]
    unit = full / largest
    row_ids = lax.broadcasted_iota(jnp.int32, full.shape, 0)
    col_ids = lax.broadcasted_iota(jnp.int32, full.shape, 1)
    identity = (row_ids == col_ids).astype(jnp.float32)
    square = sharp_dot(unit, unit)
    cube = sharp_dot(square, unit)
    low = coeffs[0] * identity + coeffs[1] * unit + coeffs[2] * square + coeffs[3] * cube
    high = coeffs[4] * unit + coeffs[5] * square + coeffs[6] * cube
    return (low + sharp_dot(cube, high)) * lax.rsqrt(jnp.sqrt(largest))


def pack_kernel(rows, *halves):
    count, fan = rows.shape
    part = halves[0].shape[0]
    spare = len(halves) * part - count
    held = jnp.concatenate([rows[...], jnp.zeros((spare, fan), jnp.float32)], axis=0)
    gap = jnp.zeros((held.shape[0], spare), jnp.float32)
    pieces = []
    for start in range(0, fan, count):
        pieces.extend([held[:, start : start + count], gap])
    packed = jnp.concatenate(pieces, axis=1).astype(jnp.bfloat16)
    for k, half in enumerate(halves):
        half[...] = packed[k * part : (k + 1) * part, :]


def flip_kernel(weight, flipped):
    lanes = weight.shape[1]
    half = lanes // 2
    low = lax.broadcasted_iota(jnp.int32, (1, lanes), 1) < half
    for j in range(weight.shape[0] // lanes):
        both = jnp.transpose(weight[j * lanes : (j + 1) * lanes, :].astype(jnp.float32))
        turned = jnp.concatenate([both[:, half:], both[:, :half]], axis=1)
        pair = (jnp.where(low, both, turned), jnp.where(low, turned, both))
        for side in range(2):
            first = (2 * j + side) * lanes
            if first < flipped.shape[0]:
                flipped[first : first + lanes, :] = pair[side].astype(jnp.bfloat16)


def add_kernel(keep, got, sent):
    sent[...] = (keep[...] + got[...].astype(jnp.float32)).astype(jnp.bfloat16)


def spread_kernel(piece, terms, spread):
    rows, lanes = terms.shape
    total = jnp.sum(terms[...].astype(jnp.float32).reshape(rows // 8, 8, lanes), axis=0)
    folded = total[:piece]
    for first in range(piece, 8, piece):
        folded = folded + total[first : first + piece]
    again = jnp.concatenate([folded] * (8 // piece), axis=0)
    spread[...] = jnp.broadcast_to(again[None], (rows // 8, 8, lanes)).reshape(rows, lanes).astype(jnp.bfloat16)


def refresh_kernel(
    place, mine, theirs, left_mine, left_theirs, right_stat, gradient, direction,
    left, spaced, tall_ref, block, powers, window,
):
    fan, width = gradient.shape
    count = direction.shape[0]
    blocks = fan // count
    step = left.shape[0] // blocks
    core = place[0]
    coeffs = root_coefficients()
    own, other = mine[...].astype(jnp.float32), theirs[...].astype(jnp.float32)
    half = own.shape[0]
    gradient[:half, :] = jnp.where(core == 0, own, other)
    gradient[half:, :] = jnp.where(core == 0, other, own)[: fan - half]
    grad_square = whole_sum(gradient[...] * gradient[...])
    for k in range(blocks):
        spaced[k * step : k * step + count, :] = gradient[k * count : (k + 1) * count, :]
        spaced[k * step + count : (k + 1) * step, :] = jnp.zeros((step - count, width), jnp.float32)
    tall = spaced[...].astype(jnp.bfloat16)
    tall_ref[...] = tall
    flat = jnp.transpose(spaced[...]).astype(jnp.bfloat16)
    right_full = DECAY * right_stat[...] + jnp.dot(flat, tall, preferred_element_type=jnp.float32)
    root = right_root_of(right_full, coeffs)
    root_high = root.astype(jnp.bfloat16)
    root_low = (root - root_high.astype(jnp.float32)).astype(jnp.bfloat16)
    parts = jnp.dot(
        jnp.concatenate([root_high, root_low], axis=0), flat, preferred_element_type=jnp.float32
    )
    carried = parts[:width] + parts[width:]
    powers[0] = carried
    vectors = block.shape[1] - width
    first_row = lax.broadcasted_iota(jnp.int32, (vectors, left.shape[0]), 0) == 0
    block[0, :width, :] = carried.astype(jnp.bfloat16)
    block[0, width:, :] = jnp.where(first_row, 1.0 / math.sqrt(fan), 0.0).astype(jnp.bfloat16)
    for source, side in ((left_mine, core), (left_theirs, 1 - core)):

        def add_gradient(turn, _, source=source, side=side):
            chip = lax.rem(place[1] // 2 + blocks // 2 - turn, blocks // 2)
            rows = pl.ds(pl.multiple_of((2 * chip + side) * step, step), step)
            outer = jnp.dot(tall_ref[rows, :], flat, preferred_element_type=jnp.float32)
            held = source[pl.ds(pl.multiple_of(turn * step, step), step), :].astype(jnp.float32)
            left[rows, :] = (DECAY * held + outer).astype(jnp.bfloat16)
            return 0

        lax.fori_loop(0, blocks // 2, add_gradient, 0)
    trace = jnp.zeros((1, 1), jnp.float32)
    for start in range(0, left.shape[0], width):
        square = left[start : start + width, start : start + width]
        trace = trace + diagonal_sum(square.astype(jnp.float32))
    inverse = 1.0 / trace
    squares = {}
    for degree in range(1, DEGREE + 1):
        product = inverse * jnp.dot(
            block[(degree - 1) % 2], left[...], preferred_element_type=jnp.float32
        )
        powers[degree] = product[:width]
        if degree < DEGREE:
            block[degree % 2] = product.astype(jnp.bfloat16)
        if degree in (POWER - 1, POWER):
            squares[degree] = whole_sum(product[width:] * product[width:])
    share = jnp.sqrt(squares[POWER]) / jnp.sqrt(squares[POWER - 1])
    update = coeffs[0] * powers[0]
    factor = 1.0 / share
    scale = factor
    for degree in range(1, DEGREE + 1):
        update = update + (coeffs[degree] * scale) * powers[degree]
        scale = scale * factor
    update = update * lax.rsqrt(jnp.sqrt(share * trace))
    powers[0] = update
    update_norm = jnp.sqrt(whole_sum(update * update))
    ratio = jnp.sqrt(grad_square) / (update_norm + 1e-06)
    span = window.shape[0]
    first = place[1] * step
    base = jnp.minimum(first // width * width, left.shape[0] - span)
    window[...] = jnp.transpose(powers[0, :, pl.ds(pl.multiple_of(base, width), span)])
    direction[...] = window[pl.ds(pl.multiple_of(first - base, 8), count), :] * ratio


def convolved(place, before, volume, after, cotangent, weight, scale, part):
    leading, depth, height, wide = volume.shape
    lanes = weight.shape[1]
    cells = wide // (lanes // 2) * (depth + 2) * height
    return pl.pallas_call(
        functools.partial(conv_kernel, scale),
        out_shape=(
            jax.ShapeDtypeStruct(cotangent.shape, jnp.bfloat16),
            jax.ShapeDtypeStruct((part, lanes), jnp.float32),
            jax.ShapeDtypeStruct((part, lanes), jnp.bfloat16),
            jax.ShapeDtypeStruct((cells, lanes), jnp.bfloat16),
        ),
        in_specs=[SMEM] + [VMEM] * 5,
        out_specs=(VMEM,) * 4,
        scratch_shapes=[pltpu.VMEM((cells, weight.shape[0]), jnp.bfloat16)],
        compiler_params=room(12),
        name="conv",
    )(place, before, volume, after, cotangent, weight)


def convolved_back(pre_grad, flipped, volume):
    leading, depth, height, wide = volume.shape
    lanes = pre_grad.shape[1]
    own = wide // (lanes // 2) * depth * height
    return pl.pallas_call(
        back_kernel,
        out_shape=jax.ShapeDtypeStruct(volume.shape, jnp.bfloat16),
        in_specs=[VMEM] * 2,
        out_specs=VMEM,
        scratch_shapes=[pltpu.VMEM((own, flipped.shape[0]), jnp.bfloat16)],
        compiler_params=room(8),
        cost_estimate=pl.CostEstimate(
            flops=2 * own * flipped.size, bytes_accessed=2 * own * flipped.shape[0], transcendentals=0
        ),
        name="conv_back",
    )(pre_grad, flipped)


def added(keep, got):
    return pl.pallas_call(
        add_kernel,
        out_shape=jax.ShapeDtypeStruct(got.shape, jnp.bfloat16),
        in_specs=[VMEM, VMEM],
        out_specs=VMEM,
        compiler_params=room(4),
        name="add",
    )(keep, got)


def summed(terms, piece):
    return pl.pallas_call(
        functools.partial(spread_kernel, piece),
        out_shape=jax.ShapeDtypeStruct(terms.shape, jnp.bfloat16),
        in_specs=[VMEM],
        out_specs=VMEM,
        compiler_params=room(4),
        name="sum",
    )(terms)


def flipped_taps(weight, taps):
    lanes = weight.shape[1]
    return pl.pallas_call(
        flip_kernel,
        out_shape=jax.ShapeDtypeStruct((taps * lanes, lanes), jnp.bfloat16),
        in_specs=[VMEM],
        out_specs=VMEM,
        compiler_params=room(8),
        name="flip",
    )(weight)


def packed_rows(rows):
    count, fan = rows.shape
    step = (count + 31) // 32 * 32
    return pl.pallas_call(
        pack_kernel,
        out_shape=(jax.ShapeDtypeStruct((step // 2, fan // count * step), jnp.bfloat16),) * 2,
        in_specs=[VMEM],
        out_specs=(VMEM,) * 2,
        compiler_params=room(16),
        name="pack",
    )(rows)


def refreshed(place, mine, theirs, left_mine, left_theirs, right_stat, fan, count):
    width = right_stat.shape[0]
    size = left_mine.shape[1]
    return pl.pallas_call(
        refresh_kernel,
        out_shape=(
            jax.ShapeDtypeStruct((fan, width), jnp.float32),
            jax.ShapeDtypeStruct((count, width), jnp.float32),
        ),
        in_specs=[SMEM] + [VMEM] * 5,
        out_specs=(VMEM, VMEM),
        scratch_shapes=[
            pltpu.VMEM((size, size), jnp.bfloat16),
            pltpu.VMEM((size, width), jnp.float32),
            pltpu.VMEM((size, width), jnp.bfloat16),
            pltpu.VMEM((2, width + 16, size), jnp.bfloat16),
            pltpu.VMEM((DEGREE + 1, width, size), jnp.float32),
            pltpu.VMEM((3 * width, width), jnp.float32),
        ],
        compiler_params=room(32),
        name="refresh",
    )(place, mine, theirs, left_mine, left_theirs, right_stat)


def per_device(volume, weight, cotangent, left_stat, right_stat):
    fan, lanes = weight.shape
    leading, depth, height, wide = volume.shape
    space = ("plane", "side")
    slabs = lax.axis_size(space)
    chips = lax.axis_size(space + ("chip",))
    swap = [(0, 1), (1, 0)]
    core = lax.axis_index("core")
    place = jnp.stack([core, lax.axis_index(("chip", "core"))])
    place = place.astype(jnp.int32)
    onward = [(i, (i + 1) % slabs) for i in range(slabs)]
    back = [((i + 1) % slabs, i) for i in range(slabs)]

    def with_plane(plane):
        return jnp.concatenate([volume, plane[..., :wide], plane[..., wide:]], axis=1)

    before = lax.ppermute(with_plane(cotangent[:, -1:]), space, onward)
    after = lax.ppermute(with_plane(cotangent[:, :1]), space, back)
    padded_fan = (fan + lanes - 1) // lanes * lanes
    padded = jnp.pad(weight, ((0, padded_fan - fan), (0, 0)))
    flipped = flipped_taps(padded, 27)
    piece = 4 * ((fan + 8 * chips - 1) // (8 * chips))
    cells = slabs * lax.axis_size(("chip", "core")) * leading * depth * height * (wide // (fan // 27))
    output, keep, give, pre_grad = convolved(
        place, before, volume, after, cotangent, padded, 1.0 / math.sqrt(cells), piece * chips
    )
    got = lax.ppermute(give, "core", swap)
    sent = added(keep, got)
    column = ("side", "chip")
    levels = lax.axis_size(column)

    def risen(rows, by):
        return lax.ppermute(rows, column, [(i, (i + by) % levels) for i in range(levels)])

    sent, own = lax.optimization_barrier((sent, packed_rows(left_stat)))
    terms = lax.all_to_all(sent.reshape(chips, piece, lanes), space + ("chip",), 0, 0)
    lower = [risen(half, 1) for half in own]
    upper = [risen(half, -1) for half in own]
    spread = summed(terms.reshape(chips * piece, lanes), piece)
    mine = lax.all_to_all(spread.reshape(chips, piece, lanes), space + ("chip",), 0, 0)
    lower[0], lower[1], upper[0], upper[1] = lax.optimization_barrier((*lower, *upper))
    far = [risen(lower[0], 1), risen(upper[1], -1)]
    input_grad = convolved_back(pre_grad, flipped, volume)
    mine, input_grad, *lefts = lax.optimization_barrier(
        (mine.reshape(chips * piece, lanes), input_grad, *own, *lower, *far, *upper)
    )
    theirs = lax.ppermute(mine, "core", swap)
    left_mine = jnp.concatenate(lefts, axis=0)
    left_theirs = lax.ppermute(left_mine, "core", swap)
    gradient, direction = refreshed(
        place, mine, theirs, left_mine, left_theirs, right_stat, fan, left_stat.shape[0]
    )
    return output, input_grad, gradient, direction


def solution(mesh):
    slabs = mesh.shape["space"]
    cut = mesh.devices.reshape(slabs // 2, 2, -1, 2)
    space, parts = ("plane", "side"), ("chip", "core")
    slab = P(parts, space, None, None)
    return jax.shard_map(
        per_device,
        mesh=Mesh(cut, space + parts),
        in_specs=(slab, P(), slab, P(parts, None), P()),
        out_specs=(slab, slab, P(), P(parts, None)),
        check_vma=False,
    )
```

```python
import functools
import math

import jax
import jax.numpy as jnp
from jax import lax
from jax.experimental import pallas as pl
from jax.experimental.pallas import tpu as pltpu
from jax.sharding import Mesh
from jax.sharding import PartitionSpec as P

POWER = 4
DEGREE = 6
DECAY = 0.9
VMEM = pl.BlockSpec(memory_space=pltpu.VMEM)
SMEM = pl.BlockSpec(memory_space=pltpu.SMEM)


def room(mebibytes):
    return pltpu.CompilerParams(vmem_limit_bytes=mebibytes * 1024 * 1024)


def offset_list():
    return [(a, b, c) for a in (-1, 0, 1) for b in (-1, 0, 1) for c in (-1, 0, 1)]


def root_coefficients():
    terms_list = [(1, 5.0), (5, -5.0), (6, 4.0)]
    coeffs = [0.0] * 7
    for degree, factor in terms_list:
        for j in range(degree + 1):
            coeffs[j] += factor * math.comb(degree, j) * 1.25 ** (degree - j) * (-0.25) ** j / 4.0
    return coeffs


def rolled_rows(cells, shift):
    if shift == 0:
        return cells
    if shift > 0:
        return jnp.concatenate([cells[:, shift:], cells[:, :shift]], axis=1)
    height = cells.shape[1]
    return jnp.concatenate([cells[:, height + shift :], cells[:, : height + shift]], axis=1)


def conv_kernel(
    scale, place, before, up, down, after, weight, out, keep, give, pre_grad, patches
):
    height = up.shape[2]
    wide = up.shape[3]
    lanes = weight.shape[1]
    half = lanes // 2
    across = wide // half
    depth = out.shape[1]
    held = depth + 2
    rows = held * height
    cells = jnp.concatenate([before[0, :2], up[0, :2], after[0, :2]], axis=0).astype(jnp.float32)
    low = lax.broadcasted_iota(jnp.int32, (1, 1, lanes), 2) < half
    low_flat = lax.broadcasted_iota(jnp.int32, (1, lanes), 1) < half
    doubled = {}
    for pair in range(across // 2):
        both = cells[:, :, pair * lanes : (pair + 1) * lanes]
        turned = jnp.concatenate([both[:, :, half:], both[:, :, :half]], axis=2)
        for side, one in enumerate((jnp.where(low, both, turned), jnp.where(low, turned, both))):
            for b in (-1, 0, 1):
                moved = rolled_rows(one, b).astype(jnp.bfloat16)
                doubled[2 * pair + side, b] = moved.reshape((held + 2) * height, lanes)

    def piece(offset):
        a, b, c = offset
        first = (1 + a) * height
        return [doubled[(x + c) % across, b][first : first + rows] for x in range(across)]

    taps = [piece(o) for o in offset_list()]
    taps.append([jnp.zeros((rows, lanes), jnp.bfloat16)] * across)
    for j in range(len(taps) // 2):
        for x in range(across):
            patches[x * rows : (x + 1) * rows, j * lanes : (j + 1) * lanes] = jnp.where(
                low_flat, taps[2 * j][x], taps[2 * j + 1][x]
            )
    preact = jnp.dot(patches[...], weight[...], preferred_element_type=jnp.float32)
    sigmoid_val = jax.nn.sigmoid(preact)
    output = (preact * sigmoid_val).astype(jnp.bfloat16)
    inner = []
    upstream = []
    for x in range(across):
        span = slice(x * lanes, (x + 1) * lanes)
        begin = (x % (across // 2)) * lanes
        side = 2 + x // (across // 2)
        for plane in (before, down, up, after):
            upstream.append(plane[0, side, :, begin : begin + lanes])
        for p in range(depth):
            first = x * rows + (1 + p) * height
            out[0, p, :, span] = output[first : first + height]
    upstream = jnp.concatenate(upstream, axis=0).astype(jnp.float32)
    slope = sigmoid_val * (1.0 + preact * (1.0 - sigmoid_val))
    grads = (upstream * slope).astype(jnp.bfloat16)
    pre_grad[...] = grads
    own = [slice(x * rows + height, x * rows + rows - height) for x in range(across)]
    own_patches = jnp.concatenate([patches[s, :] for s in own], axis=0)
    own_grads = jnp.concatenate([grads[s] for s in own], axis=0)
    local = lax.dot_general(
        own_patches, own_grads, (((0,), (0,)), ((), ())), preferred_element_type=jnp.float32
    )
    local = local * scale
    part = keep.shape[0]
    rest = jnp.zeros((2 * part - local.shape[0], lanes), jnp.float32)
    head, tail = local[:part], jnp.concatenate([local[part:], rest], axis=0)
    leading = place[0] == 0
    keep[...] = jnp.where(leading, head, tail)
    give[...] = jnp.where(leading, tail, head).astype(jnp.bfloat16)


def back_kernel(pre_grad, flipped, out, patches):
    height, depth = out.shape[2], out.shape[1]
    lanes = pre_grad.shape[1]
    across = out.shape[3] // (lanes // 2)
    rows = pre_grad.shape[0] // across
    held = rows // height
    own = depth * height
    grads = pre_grad[...].astype(jnp.float32).reshape(across, held, height, lanes)
    moved = {}
    for x in range(across):
        for b in (-1, 0, 1):
            moved[x, b] = rolled_rows(grads[x], -b).astype(jnp.bfloat16).reshape(rows, lanes)
    for k, (a, b, c) in enumerate(offset_list()):
        first = (1 - a) * height
        for x in range(across):
            patches[x * own : (x + 1) * own, k * lanes : (k + 1) * lanes] = moved[
                (x - c) % across, b
            ][first : first + own]
    result = jnp.dot(patches[...], flipped[...], preferred_element_type=jnp.float32)
    low = lax.broadcasted_iota(jnp.int32, (1, lanes), 1) < lanes // 2
    for pair in range(across // 2):
        left = result[2 * pair * own : (2 * pair + 1) * own]
        right = result[(2 * pair + 1) * own : (2 * pair + 2) * own]
        both = jnp.where(low, left, right).astype(jnp.bfloat16)
        for p in range(depth):
            out[0, p, :, pair * lanes : (pair + 1) * lanes] = both[p * height : (p + 1) * height]


def whole_sum(values):
    return jnp.sum(jnp.sum(values, axis=0, keepdims=True), axis=1, keepdims=True)


def diagonal_sum(block):
    row_ids = lax.broadcasted_iota(jnp.int32, block.shape, 0)
    col_ids = lax.broadcasted_iota(jnp.int32, block.shape, 1)
    return whole_sum(jnp.where(row_ids == col_ids, block, 0.0))


def sharp_dot(left, right):
    return jnp.dot(
        left, right, precision=lax.Precision.HIGHEST, preferred_element_type=jnp.float32
    )


def right_root_of(full, coeffs):
    size = full.shape[0]
    trace = diagonal_sum(full)
    scaled = full / trace
    vector = jnp.full((1, size), 1.0 / math.sqrt(size), jnp.float32)
    lengths = []
    for step in range(POWER):
        vector = jnp.sum(scaled * vector, axis=1 - step % 2, keepdims=True)
        lengths.append(jnp.sqrt(whole_sum(vector * vector)))
    largest = trace * lengths[POWER - 1] / lengths[POWER - 2]
    unit = full / largest
    row_ids = lax.broadcasted_iota(jnp.int32, full.shape, 0)
    col_ids = lax.broadcasted_iota(jnp.int32, full.shape, 1)
    identity = (row_ids == col_ids).astype(jnp.float32)
    square = sharp_dot(unit, unit)
    cube = sharp_dot(square, unit)
    low = coeffs[0] * identity + coeffs[1] * unit + coeffs[2] * square + coeffs[3] * cube
    high = coeffs[4] * unit + coeffs[5] * square + coeffs[6] * cube
    return (low + sharp_dot(cube, high)) * lax.rsqrt(jnp.sqrt(largest))


def message_kernel(volume, cotangent, up, down):
    depth, wide = volume.shape[1], volume.shape[3]
    for message, plane in ((up, depth - 1), (down, 0)):
        message[0, :depth] = volume[0]
        for k in range(cotangent.shape[3] // wide):
            message[0, depth + k] = cotangent[0, plane, :, k * wide : (k + 1) * wide]


def stack_kernel(*refs):
    pieces, stacked = refs[:-1], refs[-1]
    part = pieces[0].shape[0]
    for k, piece in enumerate(pieces):
        stacked[k * part : (k + 1) * part, :] = piece[...]


def pack_kernel(rows, *halves):
    count, fan = rows.shape
    part = halves[0].shape[0]
    spare = len(halves) * part - count
    held = jnp.concatenate([rows[...], jnp.zeros((spare, fan), jnp.float32)], axis=0)
    gap = jnp.zeros((held.shape[0], spare), jnp.float32)
    pieces = []
    for start in range(0, fan, count):
        pieces.extend([held[:, start : start + count], gap])
    packed = jnp.concatenate(pieces, axis=1).astype(jnp.bfloat16)
    for k, half in enumerate(halves):
        half[...] = packed[k * part : (k + 1) * part, :]


def flip_kernel(weight, flipped, padded):
    lanes = weight.shape[1]
    half = lanes // 2
    low = lax.broadcasted_iota(jnp.int32, (1, lanes), 1) < half
    spare = padded.shape[0] - weight.shape[0]
    taps = jnp.concatenate([weight[...], jnp.zeros((spare, lanes), jnp.bfloat16)], axis=0)
    padded[...] = taps
    for j in range(taps.shape[0] // lanes):
        both = jnp.transpose(taps[j * lanes : (j + 1) * lanes, :].astype(jnp.float32))
        turned = jnp.concatenate([both[:, half:], both[:, :half]], axis=1)
        pair = (jnp.where(low, both, turned), jnp.where(low, turned, both))
        for side in range(2):
            first = (2 * j + side) * lanes
            if first < flipped.shape[0]:
                flipped[first : first + lanes, :] = pair[side].astype(jnp.bfloat16)


def add_kernel(keep, got, sent):
    sent[...] = (keep[...] + got[...].astype(jnp.float32)).astype(jnp.bfloat16)


def spread_kernel(piece, terms, spread):
    rows, lanes = terms.shape
    total = jnp.sum(terms[...].astype(jnp.float32).reshape(rows // 8, 8, lanes), axis=0)
    folded = total[:piece]
    for first in range(piece, 8, piece):
        folded = folded + total[first : first + piece]
    again = jnp.concatenate([folded] * (8 // piece), axis=0)
    spread[...] = jnp.broadcast_to(again[None], (rows // 8, 8, lanes)).reshape(rows, lanes).astype(jnp.bfloat16)


def refresh_kernel(
    place, mine, theirs, left_mine, left_theirs, right_stat, gradient, direction,
    left, spaced, tall_ref, block, powers, window,
):
    fan, width = gradient.shape
    count = direction.shape[0]
    blocks = fan // count
    step = left.shape[0] // blocks
    core = place[0]
    coeffs = root_coefficients()
    own, other = mine[...].astype(jnp.float32), theirs[...].astype(jnp.float32)
    half = own.shape[0]
    gradient[:half, :] = jnp.where(core == 0, own, other)
    gradient[half:, :] = jnp.where(core == 0, other, own)[: fan - half]
    grad_square = whole_sum(gradient[...] * gradient[...])
    for k in range(blocks):
        spaced[k * step : k * step + count, :] = gradient[k * count : (k + 1) * count, :]
        spaced[k * step + count : (k + 1) * step, :] = jnp.zeros((step - count, width), jnp.float32)
    tall = spaced[...].astype(jnp.bfloat16)
    tall_ref[...] = tall
    flat = jnp.transpose(spaced[...]).astype(jnp.bfloat16)
    right_full = DECAY * right_stat[...] + jnp.dot(flat, tall, preferred_element_type=jnp.float32)
    root = right_root_of(right_full, coeffs)
    root_high = root.astype(jnp.bfloat16)
    root_low = (root - root_high.astype(jnp.float32)).astype(jnp.bfloat16)
    parts = jnp.dot(
        jnp.concatenate([root_high, root_low], axis=0), flat, preferred_element_type=jnp.float32
    )
    carried = parts[:width] + parts[width:]
    powers[0] = carried
    vectors = block.shape[1] - width
    first_row = lax.broadcasted_iota(jnp.int32, (vectors, left.shape[0]), 0) == 0
    block[0, :width, :] = carried.astype(jnp.bfloat16)
    block[0, width:, :] = jnp.where(first_row, 1.0 / math.sqrt(fan), 0.0).astype(jnp.bfloat16)
    for source, side in ((left_mine, core), (left_theirs, 1 - core)):

        def add_gradient(turn, _, source=source, side=side):
            chip = lax.rem(place[1] // 2 + blocks // 2 - turn, blocks // 2)
            rows = pl.ds(pl.multiple_of((2 * chip + side) * step, step), step)
            outer = jnp.dot(tall_ref[rows, :], flat, preferred_element_type=jnp.float32)
            held = source[pl.ds(pl.multiple_of(turn * step, step), step), :].astype(jnp.float32)
            left[rows, :] = (DECAY * held + outer).astype(jnp.bfloat16)
            return 0

        lax.fori_loop(0, blocks // 2, add_gradient, 0)
    trace = jnp.zeros((1, 1), jnp.float32)
    for start in range(0, left.shape[0], width):
        square = left[start : start + width, start : start + width]
        trace = trace + diagonal_sum(square.astype(jnp.float32))
    inverse = 1.0 / trace
    squares = {}
    for degree in range(1, DEGREE + 1):
        product = inverse * jnp.dot(
            block[(degree - 1) % 2], left[...], preferred_element_type=jnp.float32
        )
        powers[degree] = product[:width]
        if degree < DEGREE:
            block[degree % 2] = product.astype(jnp.bfloat16)
        if degree in (POWER - 1, POWER):
            squares[degree] = whole_sum(product[width:] * product[width:])
    share = jnp.sqrt(squares[POWER]) / jnp.sqrt(squares[POWER - 1])
    update = coeffs[0] * powers[0]
    factor = 1.0 / share
    scale = factor
    for degree in range(1, DEGREE + 1):
        update = update + (coeffs[degree] * scale) * powers[degree]
        scale = scale * factor
    update = update * lax.rsqrt(jnp.sqrt(share * trace))
    powers[0] = update
    update_norm = jnp.sqrt(whole_sum(update * update))
    ratio = jnp.sqrt(grad_square) / (update_norm + 1e-06)
    span = window.shape[0]
    first = place[1] * step
    base = jnp.minimum(first // width * width, left.shape[0] - span)
    window[...] = jnp.transpose(powers[0, :, pl.ds(pl.multiple_of(base, width), span)])
    direction[...] = window[pl.ds(pl.multiple_of(first - base, 8), count), :] * ratio


def convolved(place, before, up, down, after, weight, shape, scale, part):
    leading, depth, height, wide = shape
    lanes = weight.shape[1]
    cells = wide // lanes * (depth + 2) * height
    return pl.pallas_call(
        functools.partial(conv_kernel, scale),
        out_shape=(
            jax.ShapeDtypeStruct(shape, jnp.bfloat16),
            jax.ShapeDtypeStruct((part, lanes), jnp.float32),
            jax.ShapeDtypeStruct((part, lanes), jnp.bfloat16),
            jax.ShapeDtypeStruct((cells, lanes), jnp.bfloat16),
        ),
        in_specs=[SMEM] + [VMEM] * 5,
        out_specs=(VMEM,) * 4,
        scratch_shapes=[pltpu.VMEM((cells, weight.shape[0]), jnp.bfloat16)],
        compiler_params=room(12),
        name="conv",
    )(place, before, up, down, after, weight)


def convolved_back(pre_grad, flipped, volume):
    leading, depth, height, wide = volume.shape
    lanes = pre_grad.shape[1]
    own = wide // (lanes // 2) * depth * height
    return pl.pallas_call(
        back_kernel,
        out_shape=jax.ShapeDtypeStruct(volume.shape, jnp.bfloat16),
        in_specs=[VMEM] * 2,
        out_specs=VMEM,
        scratch_shapes=[pltpu.VMEM((own, flipped.shape[0]), jnp.bfloat16)],
        compiler_params=room(8),
        cost_estimate=pl.CostEstimate(
            flops=2 * own * flipped.size, bytes_accessed=2 * own * flipped.shape[0], transcendentals=0
        ),
        name="conv_back",
    )(pre_grad, flipped)


def added(keep, got):
    return pl.pallas_call(
        add_kernel,
        out_shape=jax.ShapeDtypeStruct(got.shape, jnp.bfloat16),
        in_specs=[VMEM, VMEM],
        out_specs=VMEM,
        compiler_params=room(4),
        name="add",
    )(keep, got)


def summed(terms, piece):
    return pl.pallas_call(
        functools.partial(spread_kernel, piece),
        out_shape=jax.ShapeDtypeStruct(terms.shape, jnp.bfloat16),
        in_specs=[VMEM],
        out_specs=VMEM,
        compiler_params=room(4),
        name="sum",
    )(terms)


def flipped_taps(weight, taps):
    fan, lanes = weight.shape
    return pl.pallas_call(
        flip_kernel,
        out_shape=(
            jax.ShapeDtypeStruct((taps * lanes, lanes), jnp.bfloat16),
            jax.ShapeDtypeStruct(((fan + lanes - 1) // lanes * lanes, lanes), jnp.bfloat16),
        ),
        in_specs=[VMEM],
        out_specs=(VMEM,) * 2,
        compiler_params=room(8),
        name="flip",
    )(weight)


def messages(volume, cotangent):
    leading, depth, height, wide = volume.shape
    shape = (leading, depth + cotangent.shape[3] // wide, height, wide)
    return pl.pallas_call(
        message_kernel,
        out_shape=(jax.ShapeDtypeStruct(shape, jnp.bfloat16),) * 2,
        in_specs=[VMEM] * 2,
        out_specs=(VMEM,) * 2,
        compiler_params=room(4),
        name="messages",
    )(volume, cotangent)


def stacked_rows(pieces):
    rows, size = pieces[0].shape
    return pl.pallas_call(
        stack_kernel,
        out_shape=jax.ShapeDtypeStruct((rows * len(pieces), size), pieces[0].dtype),
        in_specs=[VMEM] * len(pieces),
        out_specs=VMEM,
        compiler_params=room(4),
        name="stack",
    )(*pieces)


def packed_rows(rows):
    count, fan = rows.shape
    step = (count + 31) // 32 * 32
    return pl.pallas_call(
        pack_kernel,
        out_shape=(jax.ShapeDtypeStruct((step // 2, fan // count * step), jnp.bfloat16),) * 2,
        in_specs=[VMEM],
        out_specs=(VMEM,) * 2,
        compiler_params=room(16),
        name="pack",
    )(rows)


def refreshed(place, mine, theirs, left_mine, left_theirs, right_stat, fan, count):
    width = right_stat.shape[0]
    size = left_mine.shape[1]
    return pl.pallas_call(
        refresh_kernel,
        out_shape=(
            jax.ShapeDtypeStruct((fan, width), jnp.float32),
            jax.ShapeDtypeStruct((count, width), jnp.float32),
        ),
        in_specs=[SMEM] + [VMEM] * 5,
        out_specs=(VMEM, VMEM),
        scratch_shapes=[
            pltpu.VMEM((size, size), jnp.bfloat16),
            pltpu.VMEM((size, width), jnp.float32),
            pltpu.VMEM((size, width), jnp.bfloat16),
            pltpu.VMEM((2, width + 16, size), jnp.bfloat16),
            pltpu.VMEM((DEGREE + 1, width, size), jnp.float32),
            pltpu.VMEM((3 * width, width), jnp.float32),
        ],
        compiler_params=room(32),
        name="refresh",
    )(place, mine, theirs, left_mine, left_theirs, right_stat)


def per_device(volume, weight, cotangent, left_stat, right_stat):
    fan, lanes = weight.shape
    leading, depth, height, wide = volume.shape
    space = ("plane", "side")
    slabs = lax.axis_size(space)
    chips = lax.axis_size(space + ("chip",))
    swap = [(0, 1), (1, 0)]
    core = lax.axis_index("core")
    place = jnp.stack([core, lax.axis_index(("chip", "core"))])
    place = place.astype(jnp.int32)
    onward = [(i, (i + 1) % slabs) for i in range(slabs)]
    back = [((i + 1) % slabs, i) for i in range(slabs)]

    up, down = messages(volume, cotangent)
    before = lax.ppermute(up, space, onward)
    after = lax.ppermute(down, space, back)
    flipped, padded = flipped_taps(weight, 27)
    piece = 4 * ((fan + 8 * chips - 1) // (8 * chips))
    cells = slabs * lax.axis_size(("chip", "core")) * leading * depth * height * (wide // (fan // 27))
    output, keep, give, pre_grad = convolved(
        place, before, up, down, after, padded, cotangent.shape, 1.0 / math.sqrt(cells), piece * chips
    )
    got = lax.ppermute(give, "core", swap)
    sent = added(keep, got)
    column = ("side", "chip")
    levels = lax.axis_size(column)

    def risen(rows, by):
        return lax.ppermute(rows, column, [(i, (i + by) % levels) for i in range(levels)])

    sent, own = lax.optimization_barrier((sent, packed_rows(left_stat)))
    terms = lax.all_to_all(sent.reshape(chips, piece, lanes), space + ("chip",), 0, 0)
    lower = [risen(half, 1) for half in own]
    upper = [risen(half, -1) for half in own]
    spread = summed(terms.reshape(chips * piece, lanes), piece)
    mine = lax.all_to_all(spread.reshape(chips, piece, lanes), space + ("chip",), 0, 0)
    lower[0], lower[1], upper[0], upper[1] = lax.optimization_barrier((*lower, *upper))
    far = [risen(lower[0], 1), risen(upper[1], -1)]
    input_grad = convolved_back(pre_grad, flipped, volume)
    mine = mine.reshape(chips * piece, lanes)
    _, *lefts = lax.optimization_barrier((mine, *own, *lower, *far, *upper))
    mine, input_grad = lax.optimization_barrier((mine, input_grad))
    theirs = lax.ppermute(mine, "core", swap)
    left_mine = stacked_rows(lefts)
    left_theirs = lax.ppermute(left_mine, "core", swap)
    gradient, direction = refreshed(
        place, mine, theirs, left_mine, left_theirs, right_stat, fan, left_stat.shape[0]
    )
    return output, input_grad, gradient, direction


def solution(mesh):
    slabs = mesh.shape["space"]
    cut = mesh.devices.reshape(slabs // 2, 2, -1, 2)
    space, parts = ("plane", "side"), ("chip", "core")
    slab = P(parts, space, None, None)
    return jax.shard_map(
        per_device,
        mesh=Mesh(cut, space + parts),
        in_specs=(slab, P(), slab, P(parts, None), P()),
        out_specs=(slab, slab, P(), P(parts, None)),
        check_vma=False,
    )
```

```python
import functools
import math

import jax
import jax.numpy as jnp
from jax import lax
from jax.experimental import pallas as pl
from jax.experimental.pallas import tpu as pltpu
from jax.sharding import Mesh
from jax.sharding import PartitionSpec as P

POWER = 4
DEGREE = 6
DECAY = 0.9
VMEM = pl.BlockSpec(memory_space=pltpu.VMEM)
SMEM = pl.BlockSpec(memory_space=pltpu.SMEM)


def room(mebibytes):
    return pltpu.CompilerParams(vmem_limit_bytes=mebibytes * 1024 * 1024)


def offset_list():
    return [(a, b, c) for a in (-1, 0, 1) for b in (-1, 0, 1) for c in (-1, 0, 1)]


def root_coefficients():
    terms_list = [(1, 5.0), (5, -5.0), (6, 4.0)]
    coeffs = [0.0] * 7
    for degree, factor in terms_list:
        for j in range(degree + 1):
            coeffs[j] += factor * math.comb(degree, j) * 1.25 ** (degree - j) * (-0.25) ** j / 4.0
    return coeffs


def rolled_rows(cells, shift):
    if shift == 0:
        return cells
    if shift > 0:
        return jnp.concatenate([cells[:, shift:], cells[:, :shift]], axis=1)
    height = cells.shape[1]
    return jnp.concatenate([cells[:, height + shift :], cells[:, : height + shift]], axis=1)


def conv_kernel(
    scale, place, before, up, down, after, weight, flipped,
    out, keep, give, input_grad, patches, pre_grad, back_patches,
):
    height = up.shape[2]
    wide = up.shape[3]
    lanes = weight.shape[1]
    half = lanes // 2
    across = wide // half
    depth = out.shape[1]
    held = depth + 2
    rows = held * height
    cells = jnp.concatenate([before[0, :2], up[0, :2], after[0, :2]], axis=0).astype(jnp.float32)
    low = lax.broadcasted_iota(jnp.int32, (1, 1, lanes), 2) < half
    low_flat = lax.broadcasted_iota(jnp.int32, (1, lanes), 1) < half
    doubled = {}
    for pair in range(across // 2):
        both = cells[:, :, pair * lanes : (pair + 1) * lanes]
        turned = jnp.concatenate([both[:, :, half:], both[:, :, :half]], axis=2)
        for side, one in enumerate((jnp.where(low, both, turned), jnp.where(low, turned, both))):
            for b in (-1, 0, 1):
                moved = rolled_rows(one, b).astype(jnp.bfloat16)
                doubled[2 * pair + side, b] = moved.reshape((held + 2) * height, lanes)

    def piece(offset):
        a, b, c = offset
        first = (1 + a) * height
        return [doubled[(x + c) % across, b][first : first + rows] for x in range(across)]

    taps = [piece(o) for o in offset_list()]
    taps.append([jnp.zeros((rows, lanes), jnp.bfloat16)] * across)
    for j in range(len(taps) // 2):
        for x in range(across):
            patches[x * rows : (x + 1) * rows, j * lanes : (j + 1) * lanes] = jnp.where(
                low_flat, taps[2 * j][x], taps[2 * j + 1][x]
            )
    preact = jnp.dot(patches[...], weight[...], preferred_element_type=jnp.float32)
    sigmoid_val = jax.nn.sigmoid(preact)
    output = (preact * sigmoid_val).astype(jnp.bfloat16)
    inner = []
    upstream = []
    for x in range(across):
        span = slice(x * lanes, (x + 1) * lanes)
        begin = (x % (across // 2)) * lanes
        side = 2 + x // (across // 2)
        for plane in (before, down, up, after):
            upstream.append(plane[0, side, :, begin : begin + lanes])
        for p in range(depth):
            first = x * rows + (1 + p) * height
            out[0, p, :, span] = output[first : first + height]
    upstream = jnp.concatenate(upstream, axis=0).astype(jnp.float32)
    slope = sigmoid_val * (1.0 + preact * (1.0 - sigmoid_val))
    grads = (upstream * slope).astype(jnp.bfloat16)
    pre_grad[...] = grads
    own = [slice(x * rows + height, x * rows + rows - height) for x in range(across)]
    own_patches = jnp.concatenate([patches[s, :] for s in own], axis=0)
    own_grads = jnp.concatenate([grads[s] for s in own], axis=0)
    local = lax.dot_general(
        own_patches, own_grads, (((0,), (0,)), ((), ())), preferred_element_type=jnp.float32
    )
    local = local * scale
    part = keep.shape[0]
    rest = jnp.zeros((2 * part - local.shape[0], lanes), jnp.float32)
    head, tail = local[:part], jnp.concatenate([local[part:], rest], axis=0)
    leading = place[0] == 0
    keep[...] = jnp.where(leading, head, tail)
    give[...] = jnp.where(leading, tail, head).astype(jnp.bfloat16)
    back_kernel(pre_grad, flipped, input_grad, back_patches)


def back_kernel(pre_grad, flipped, out, patches):
    height, depth = out.shape[2], out.shape[1]
    lanes = pre_grad.shape[1]
    across = out.shape[3] // (lanes // 2)
    rows = pre_grad.shape[0] // across
    held = rows // height
    own = depth * height
    grads = pre_grad[...].astype(jnp.float32).reshape(across, held, height, lanes)
    moved = {}
    for x in range(across):
        for b in (-1, 0, 1):
            moved[x, b] = rolled_rows(grads[x], -b).astype(jnp.bfloat16).reshape(rows, lanes)
    for k, (a, b, c) in enumerate(offset_list()):
        first = (1 - a) * height
        for x in range(across):
            patches[x * own : (x + 1) * own, k * lanes : (k + 1) * lanes] = moved[
                (x - c) % across, b
            ][first : first + own]
    result = jnp.dot(patches[...], flipped[...], preferred_element_type=jnp.float32)
    low = lax.broadcasted_iota(jnp.int32, (1, lanes), 1) < lanes // 2
    for pair in range(across // 2):
        left = result[2 * pair * own : (2 * pair + 1) * own]
        right = result[(2 * pair + 1) * own : (2 * pair + 2) * own]
        both = jnp.where(low, left, right).astype(jnp.bfloat16)
        for p in range(depth):
            out[0, p, :, pair * lanes : (pair + 1) * lanes] = both[p * height : (p + 1) * height]


def whole_sum(values):
    return jnp.sum(jnp.sum(values, axis=0, keepdims=True), axis=1, keepdims=True)


def diagonal_sum(block):
    row_ids = lax.broadcasted_iota(jnp.int32, block.shape, 0)
    col_ids = lax.broadcasted_iota(jnp.int32, block.shape, 1)
    return whole_sum(jnp.where(row_ids == col_ids, block, 0.0))


def sharp_dot(left, right):
    return jnp.dot(
        left, right, precision=lax.Precision.HIGHEST, preferred_element_type=jnp.float32
    )


def right_root_of(full, coeffs):
    size = full.shape[0]
    trace = diagonal_sum(full)
    scaled = full / trace
    vector = jnp.full((1, size), 1.0 / math.sqrt(size), jnp.float32)
    lengths = []
    for step in range(POWER):
        vector = jnp.sum(scaled * vector, axis=1 - step % 2, keepdims=True)
        lengths.append(jnp.sqrt(whole_sum(vector * vector)))
    largest = trace * lengths[POWER - 1] / lengths[POWER - 2]
    unit = full / largest
    row_ids = lax.broadcasted_iota(jnp.int32, full.shape, 0)
    col_ids = lax.broadcasted_iota(jnp.int32, full.shape, 1)
    identity = (row_ids == col_ids).astype(jnp.float32)
    square = sharp_dot(unit, unit)
    cube = sharp_dot(square, unit)
    low = coeffs[0] * identity + coeffs[1] * unit + coeffs[2] * square + coeffs[3] * cube
    high = coeffs[4] * unit + coeffs[5] * square + coeffs[6] * cube
    return (low + sharp_dot(cube, high)) * lax.rsqrt(jnp.sqrt(largest))


def message_kernel(volume, cotangent, up, down):
    depth, wide = volume.shape[1], volume.shape[3]
    for message, plane in ((up, depth - 1), (down, 0)):
        message[0, :depth] = volume[0]
        for k in range(cotangent.shape[3] // wide):
            message[0, depth + k] = cotangent[0, plane, :, k * wide : (k + 1) * wide]


def stack_kernel(*refs):
    pieces, stacked = refs[:-1], refs[-1]
    part = pieces[0].shape[0]
    for k, piece in enumerate(pieces):
        stacked[k * part : (k + 1) * part, :] = piece[...]


def pack_kernel(rows, *halves):
    count, fan = rows.shape
    part = halves[0].shape[0]
    spare = len(halves) * part - count
    held = jnp.concatenate([rows[...], jnp.zeros((spare, fan), jnp.float32)], axis=0)
    gap = jnp.zeros((held.shape[0], spare), jnp.float32)
    pieces = []
    for start in range(0, fan, count):
        pieces.extend([held[:, start : start + count], gap])
    packed = jnp.concatenate(pieces, axis=1).astype(jnp.bfloat16)
    for k, half in enumerate(halves):
        half[...] = packed[k * part : (k + 1) * part, :]


def flip_kernel(weight, flipped, padded):
    lanes = weight.shape[1]
    half = lanes // 2
    low = lax.broadcasted_iota(jnp.int32, (1, lanes), 1) < half
    spare = padded.shape[0] - weight.shape[0]
    taps = jnp.concatenate([weight[...], jnp.zeros((spare, lanes), jnp.bfloat16)], axis=0)
    padded[...] = taps
    for j in range(taps.shape[0] // lanes):
        both = jnp.transpose(taps[j * lanes : (j + 1) * lanes, :].astype(jnp.float32))
        turned = jnp.concatenate([both[:, half:], both[:, :half]], axis=1)
        pair = (jnp.where(low, both, turned), jnp.where(low, turned, both))
        for side in range(2):
            first = (2 * j + side) * lanes
            if first < flipped.shape[0]:
                flipped[first : first + lanes, :] = pair[side].astype(jnp.bfloat16)


def add_kernel(keep, got, sent):
    sent[...] = (keep[...] + got[...].astype(jnp.float32)).astype(jnp.bfloat16)


def spread_kernel(piece, terms, spread):
    rows, lanes = terms.shape
    total = jnp.sum(terms[...].astype(jnp.float32).reshape(rows // 8, 8, lanes), axis=0)
    folded = total[:piece]
    for first in range(piece, 8, piece):
        folded = folded + total[first : first + piece]
    again = jnp.concatenate([folded] * (8 // piece), axis=0)
    spread[...] = jnp.broadcast_to(again[None], (rows // 8, 8, lanes)).reshape(rows, lanes).astype(jnp.bfloat16)


def refresh_kernel(
    place, mine, theirs, left_mine, left_theirs, right_stat, gradient, direction,
    left, spaced, tall_ref, block, powers, window,
):
    fan, width = gradient.shape
    count = direction.shape[0]
    blocks = fan // count
    step = left.shape[0] // blocks
    core = place[0]
    coeffs = root_coefficients()
    own, other = mine[...].astype(jnp.float32), theirs[...].astype(jnp.float32)
    half = own.shape[0]
    gradient[:half, :] = jnp.where(core == 0, own, other)
    gradient[half:, :] = jnp.where(core == 0, other, own)[: fan - half]
    grad_square = whole_sum(gradient[...] * gradient[...])
    for k in range(blocks):
        spaced[k * step : k * step + count, :] = gradient[k * count : (k + 1) * count, :]
        spaced[k * step + count : (k + 1) * step, :] = jnp.zeros((step - count, width), jnp.float32)
    tall = spaced[...].astype(jnp.bfloat16)
    tall_ref[...] = tall
    flat = jnp.transpose(spaced[...]).astype(jnp.bfloat16)
    right_full = DECAY * right_stat[...] + jnp.dot(flat, tall, preferred_element_type=jnp.float32)
    root = right_root_of(right_full, coeffs)
    root_high = root.astype(jnp.bfloat16)
    root_low = (root - root_high.astype(jnp.float32)).astype(jnp.bfloat16)
    parts = jnp.dot(
        jnp.concatenate([root_high, root_low], axis=0), flat, preferred_element_type=jnp.float32
    )
    carried = parts[:width] + parts[width:]
    powers[0] = carried
    vectors = block.shape[1] - width
    first_row = lax.broadcasted_iota(jnp.int32, (vectors, left.shape[0]), 0) == 0
    block[0, :width, :] = carried.astype(jnp.bfloat16)
    block[0, width:, :] = jnp.where(first_row, 1.0 / math.sqrt(fan), 0.0).astype(jnp.bfloat16)
    for source, side in ((left_mine, core), (left_theirs, 1 - core)):

        def add_gradient(turn, _, source=source, side=side):
            chip = lax.rem(place[1] // 2 + blocks // 2 - turn, blocks // 2)
            rows = pl.ds(pl.multiple_of((2 * chip + side) * step, step), step)
            outer = jnp.dot(tall_ref[rows, :], flat, preferred_element_type=jnp.float32)
            held = source[pl.ds(pl.multiple_of(turn * step, step), step), :].astype(jnp.float32)
            left[rows, :] = (DECAY * held + outer).astype(jnp.bfloat16)
            return 0

        lax.fori_loop(0, blocks // 2, add_gradient, 0)
    trace = jnp.zeros((1, 1), jnp.float32)
    for start in range(0, left.shape[0], width):
        square = left[start : start + width, start : start + width]
        trace = trace + diagonal_sum(square.astype(jnp.float32))
    inverse = 1.0 / trace
    squares = {}
    for degree in range(1, DEGREE + 1):
        product = inverse * jnp.dot(
            block[(degree - 1) % 2], left[...], preferred_element_type=jnp.float32
        )
        powers[degree] = product[:width]
        if degree < DEGREE:
            block[degree % 2] = product.astype(jnp.bfloat16)
        if degree in (POWER - 1, POWER):
            squares[degree] = whole_sum(product[width:] * product[width:])
    share = jnp.sqrt(squares[POWER]) / jnp.sqrt(squares[POWER - 1])
    update = coeffs[0] * powers[0]
    factor = 1.0 / share
    scale = factor
    for degree in range(1, DEGREE + 1):
        update = update + (coeffs[degree] * scale) * powers[degree]
        scale = scale * factor
    update = update * lax.rsqrt(jnp.sqrt(share * trace))
    powers[0] = update
    update_norm = jnp.sqrt(whole_sum(update * update))
    ratio = jnp.sqrt(grad_square) / (update_norm + 1e-06)
    span = window.shape[0]
    first = place[1] * step
    base = jnp.minimum(first // width * width, left.shape[0] - span)
    window[...] = jnp.transpose(powers[0, :, pl.ds(pl.multiple_of(base, width), span)])
    direction[...] = window[pl.ds(pl.multiple_of(first - base, 8), count), :] * ratio


def convolved(place, before, up, down, after, weight, flipped, shape, scale, part):
    leading, depth, height, wide = shape
    lanes = weight.shape[1]
    across = wide // lanes
    cells, own = across * (depth + 2) * height, across * depth * height
    return pl.pallas_call(
        functools.partial(conv_kernel, scale),
        out_shape=(
            jax.ShapeDtypeStruct(shape, jnp.bfloat16),
            jax.ShapeDtypeStruct((part, lanes), jnp.float32),
            jax.ShapeDtypeStruct((part, lanes), jnp.bfloat16),
            jax.ShapeDtypeStruct((leading, depth, height, wide // 2), jnp.bfloat16),
        ),
        in_specs=[SMEM] + [VMEM] * 6,
        out_specs=(VMEM,) * 4,
        scratch_shapes=[
            pltpu.VMEM((cells, weight.shape[0]), jnp.bfloat16),
            pltpu.VMEM((cells, lanes), jnp.bfloat16),
            pltpu.VMEM((own, flipped.shape[0]), jnp.bfloat16),
        ],
        compiler_params=room(12),
        name="conv",
    )(place, before, up, down, after, weight, flipped)


def added(keep, got):
    return pl.pallas_call(
        add_kernel,
        out_shape=jax.ShapeDtypeStruct(got.shape, jnp.bfloat16),
        in_specs=[VMEM, VMEM],
        out_specs=VMEM,
        compiler_params=room(4),
        name="add",
    )(keep, got)


def summed(terms, piece):
    return pl.pallas_call(
        functools.partial(spread_kernel, piece),
        out_shape=jax.ShapeDtypeStruct(terms.shape, jnp.bfloat16),
        in_specs=[VMEM],
        out_specs=VMEM,
        compiler_params=room(4),
        name="sum",
    )(terms)


def flipped_taps(weight, taps):
    fan, lanes = weight.shape
    return pl.pallas_call(
        flip_kernel,
        out_shape=(
            jax.ShapeDtypeStruct((taps * lanes, lanes), jnp.bfloat16),
            jax.ShapeDtypeStruct(((fan + lanes - 1) // lanes * lanes, lanes), jnp.bfloat16),
        ),
        in_specs=[VMEM],
        out_specs=(VMEM,) * 2,
        compiler_params=room(8),
        name="flip",
    )(weight)


def messages(volume, cotangent):
    leading, depth, height, wide = volume.shape
    shape = (leading, depth + cotangent.shape[3] // wide, height, wide)
    return pl.pallas_call(
        message_kernel,
        out_shape=(jax.ShapeDtypeStruct(shape, jnp.bfloat16),) * 2,
        in_specs=[VMEM] * 2,
        out_specs=(VMEM,) * 2,
        compiler_params=room(4),
        name="messages",
    )(volume, cotangent)


def stacked_rows(pieces):
    rows, size = pieces[0].shape
    return pl.pallas_call(
        stack_kernel,
        out_shape=jax.ShapeDtypeStruct((rows * len(pieces), size), pieces[0].dtype),
        in_specs=[VMEM] * len(pieces),
        out_specs=VMEM,
        compiler_params=room(4),
        name="stack",
    )(*pieces)


def packed_rows(rows):
    count, fan = rows.shape
    step = (count + 31) // 32 * 32
    return pl.pallas_call(
        pack_kernel,
        out_shape=(jax.ShapeDtypeStruct((step // 2, fan // count * step), jnp.bfloat16),) * 2,
        in_specs=[VMEM],
        out_specs=(VMEM,) * 2,
        compiler_params=room(16),
        name="pack",
    )(rows)


def refreshed(place, mine, theirs, left_mine, left_theirs, right_stat, fan, count):
    width = right_stat.shape[0]
    size = left_mine.shape[1]
    return pl.pallas_call(
        refresh_kernel,
        out_shape=(
            jax.ShapeDtypeStruct((fan, width), jnp.float32),
            jax.ShapeDtypeStruct((count, width), jnp.float32),
        ),
        in_specs=[SMEM] + [VMEM] * 5,
        out_specs=(VMEM, VMEM),
        scratch_shapes=[
            pltpu.VMEM((size, size), jnp.bfloat16),
            pltpu.VMEM((size, width), jnp.float32),
            pltpu.VMEM((size, width), jnp.bfloat16),
            pltpu.VMEM((2, width + 16, size), jnp.bfloat16),
            pltpu.VMEM((DEGREE + 1, width, size), jnp.float32),
            pltpu.VMEM((3 * width, width), jnp.float32),
        ],
        compiler_params=room(32),
        name="refresh",
    )(place, mine, theirs, left_mine, left_theirs, right_stat)


def per_device(volume, weight, cotangent, left_stat, right_stat):
    fan, lanes = weight.shape
    leading, depth, height, wide = volume.shape
    space = ("plane", "side")
    slabs = lax.axis_size(space)
    chips = lax.axis_size(space + ("chip",))
    swap = [(0, 1), (1, 0)]
    core = lax.axis_index("core")
    place = jnp.stack([core, lax.axis_index(("chip", "core"))])
    place = place.astype(jnp.int32)
    onward = [(i, (i + 1) % slabs) for i in range(slabs)]
    back = [((i + 1) % slabs, i) for i in range(slabs)]

    up, down = messages(volume, cotangent)
    before = lax.ppermute(up, space, onward)
    after = lax.ppermute(down, space, back)
    flipped, padded = flipped_taps(weight, 27)
    piece = 4 * ((fan + 8 * chips - 1) // (8 * chips))
    cells = slabs * lax.axis_size(("chip", "core")) * leading * depth * height * (wide // (fan // 27))
    output, keep, give, input_grad = convolved(
        place, before, up, down, after, padded, flipped, cotangent.shape, 1.0 / math.sqrt(cells), piece * chips
    )
    got = lax.ppermute(give, "core", swap)
    sent = added(keep, got)
    column = ("side", "chip")
    levels = lax.axis_size(column)

    def risen(rows, by):
        return lax.ppermute(rows, column, [(i, (i + by) % levels) for i in range(levels)])

    sent, own = lax.optimization_barrier((sent, packed_rows(left_stat)))
    terms = lax.all_to_all(sent.reshape(chips, piece, lanes), space + ("chip",), 0, 0)
    lower = [risen(half, 1) for half in own]
    upper = [risen(half, -1) for half in own]
    spread = summed(terms.reshape(chips * piece, lanes), piece)
    mine = lax.all_to_all(spread.reshape(chips, piece, lanes), space + ("chip",), 0, 0)
    lower[0], lower[1], upper[0], upper[1] = lax.optimization_barrier((*lower, *upper))
    far = [risen(lower[0], 1), risen(upper[1], -1)]
    mine = mine.reshape(chips * piece, lanes)
    _, *lefts = lax.optimization_barrier((mine, *own, *lower, *far, *upper))
    theirs = lax.ppermute(mine, "core", swap)
    left_mine = stacked_rows(lefts)
    left_theirs = lax.ppermute(left_mine, "core", swap)
    gradient, direction = refreshed(
        place, mine, theirs, left_mine, left_theirs, right_stat, fan, left_stat.shape[0]
    )
    return output, input_grad, gradient, direction


def solution(mesh):
    slabs = mesh.shape["space"]
    cut = mesh.devices.reshape(slabs // 2, 2, -1, 2)
    space, parts = ("plane", "side"), ("chip", "core")
    slab = P(parts, space, None, None)
    return jax.shard_map(
        per_device,
        mesh=Mesh(cut, space + parts),
        in_specs=(slab, P(), slab, P(parts, None), P()),
        out_specs=(slab, slab, P(), P(parts, None)),
        check_vma=False,
    )
```
